32 devices in a mesh: groups: 2 (over y), ex: 8 (over z, x), layer: 2 (over core).
Axes of the slice: x: 2, y: 2, z: 4, core: 2. Of those that a mesh axis runs over, the one named last changes fastest.
Arguments:
- query_out_grads: bfloat16 [2, 32, 7168], P('layer', ('groups', 'ex')), parts along dimension 1, may hold values from -6 to 6
- query_inputs: bfloat16 [2, 32, 4096], P('layer', ('groups', 'ex')), parts along dimension 1, may hold values from -6 to 6
- train_out_grads: bfloat16 [2, 2560, 7168], P('layer', ('groups', 'ex')), parts along dimension 1, may hold values from -0.0625 to 0.0625
- train_inputs: bfloat16 [2, 2560, 4096], P('layer', ('groups', 'ex')), parts along dimension 1, may hold values from -0.09375 to 0.09375
- basis_hidden: bfloat16 [2, 7168, 7168], P('layer', None, 'ex'), may hold values from -0.0625 to 0.0625
- basis_inputs: bfloat16 [2, 4096, 4096], P('layer', None, 'ex'), may hold values from -0.09375 to 0.09375
- eig_hidden: float32 [2, 7168], P('layer'), may hold values from 0.5 to 5
- eig_inputs: float32 [2, 4096], P('layer'), may hold values from 0.5 to 5
- query_ids: int32 [32], P('groups'), parts along dimension 0, may hold values from 0 to 7, as said below
- example_ids: int32 [16, 160], P(('groups', 'ex')), parts along dimension 0, may hold values from 0 to 1, as said below
Outputs:
- relative_scores: float32 [16, 16], P(('groups', 'layer'), 'ex'), parts along dimension 0
The draws below stay inside these ranges and needn't reach their ends.
There are 2 independent parts, one for each index of `groups`. The reference program is written for one: setup_inputs(seed, part) draws one part's arguments, and reference() takes and returns one part's arrays. A program takes and returns all parts, laid end to end along the dimension named above; an argument that names none is the same for every part. Nothing has to cross between parts.
Inputs may be any that keep to these rules, and one draw needn't show every extreme that they name: `query_ids`: never falls along the tokens; every query owns one token or more. `example_ids`: never falls along each row; every number appears in every row.
All inputs are finite; a program needn't handle non-finite values.
Results may differ from the reference program's by a relative error of at most 0.0045.
Values may be sent and summed in bfloat16 or wider, within the bound.
No kernel may reach another device: no remote copies, remote signals or barrier semaphores. Data moves between devices by JAX's collectives and lax.ppermute only.
A program may use at most 64 MiB of HBM per device.

```python
import math
import jax
import jax.numpy as jnp
from jax import lax

D = 4096
FFW = 7168
QT_DEV = 2
ET_DEV = 160
E_DEV = 2
QUERIES = 8
LAYERS = 2
QTOK = 16
ETOK = 1280
EXAMPLES = 16
N_EX = 8


def segment_ids(key, positions, count):
    boundary = jax.random.permutation(key, positions - 1)[:count - 1] + 1
    position = jnp.arange(positions, dtype=jnp.int32)
    return jnp.sum((position[:, None] >= boundary[None, :]).astype(jnp.int32), axis=1).astype(jnp.int32)


def draw_query_ids(key, part):
    key = jax.random.fold_in(key, 11)
    return segment_ids(key, QT_DEV * N_EX, QUERIES)


def draw_example_ids(key, part):
    key = jax.random.fold_in(key, 23)
    row_keys = jax.random.split(key, N_EX)
    return jax.vmap(lambda row_key: segment_ids(row_key, ET_DEV, E_DEV))(row_keys)


def block_scale(own_key, extent, shards, smallest, top_value):
    factor_of = 1.0
    for axis_at, blocks in shards:
        draws = jax.random.uniform(jax.random.fold_in(jax.random.fold_in(own_key, 6), axis_at), (blocks,), jnp.float32, smallest / len(shards), top_value / len(shards))
        factor_of = factor_of * jnp.repeat(jnp.exp(draws), extent[axis_at] // blocks).reshape((-1,) + (1,) * (len(extent) - 1 - axis_at))
    return factor_of


def normal_values(own_key, shape, deviation, limit, cuts=(), held_as=jnp.bfloat16):
    gain = block_scale(own_key, shape, cuts, -0.22, 0.18) if cuts else 1.0
    values = jax.random.normal(own_key, shape, jnp.float32) * deviation * gain
    return jnp.minimum(jnp.maximum(values, -limit), limit).astype(held_as)


def setup_inputs(seed: int = 0, part: int = 0) -> dict:
    key_of = jax.random.split(jax.random.key(seed), 11)
    own_keys = jax.random.split(jax.random.fold_in(key_of[10], part), 11)
    return {
        "query_out_grads": normal_values(own_keys[0], (LAYERS, QTOK, FFW), 1.0, 6.0, ((0, 2), (1, 8))),
        "query_inputs": normal_values(own_keys[1], (LAYERS, QTOK, D), 1.0, 6.0, ((0, 2), (1, 8))),
        "train_out_grads": normal_values(own_keys[2], (LAYERS, ETOK, FFW), FFW ** -0.5, 0.0625, ((0, 2), (1, 8))),
        "train_inputs": normal_values(own_keys[3], (LAYERS, ETOK, D), D ** -0.5, 0.09375, ((0, 2), (1, 8))),
        "basis_hidden": normal_values(key_of[4], (LAYERS, FFW, FFW), FFW ** -0.5, 0.0625, ((0, 2), (2, 8))),
        "basis_inputs": normal_values(key_of[5], (LAYERS, D, D), D ** -0.5, 0.09375, ((0, 2), (2, 8))),
        "eig_hidden": jnp.clip(jnp.exp(math.log(5.0) - 2.3025851 * jax.random.uniform(key_of[6], (LAYERS, FFW), jnp.float32) ** block_scale(key_of[6], (LAYERS, FFW), ((0, 2),), -0.2, 0.2)), 0.5, 5.0),
        "eig_inputs": jnp.clip(jnp.exp(math.log(5.0) - 2.3025851 * jax.random.uniform(key_of[7], (LAYERS, D), jnp.float32) ** block_scale(key_of[7], (LAYERS, D), ((0, 2),), -0.2, 0.2)), 0.5, 5.0),
        "query_ids": draw_query_ids(jax.random.fold_in(jax.random.fold_in(key_of[10], part), 71), part),
        "example_ids": draw_example_ids(jax.random.fold_in(jax.random.fold_in(key_of[10], part), 71), part),
    }


DAMP = 0.1

def reference(query_out_grads, query_inputs, train_out_grads, train_inputs, basis_hidden, basis_inputs, eig_hidden, eig_inputs, query_ids, example_ids):
    query_hot = (query_ids[None, :] == jnp.arange(QUERIES, dtype=jnp.int32)[:, None]).astype(jnp.float32)
    example_hot = (example_ids[:, None, :] == jnp.arange(E_DEV, dtype=jnp.int32)[None, :, None]).astype(jnp.float32)
    pair_scores = jnp.zeros((N_EX, QUERIES, E_DEV), jnp.float32)
    self_influence = jnp.zeros((N_EX, E_DEV), jnp.float32)
    for layer_index in range(LAYERS):
        gain_hidden = 1.0 / (eig_hidden[layer_index] + DAMP)
        gain_inputs = 1.0 / (eig_inputs[layer_index] + DAMP)
        rot_hidden = (jnp.dot(query_out_grads[layer_index], basis_hidden[layer_index], preferred_element_type=jnp.float32) * gain_hidden).astype(jnp.bfloat16)
        rot_inputs = (jnp.dot(query_inputs[layer_index], basis_inputs[layer_index], preferred_element_type=jnp.float32) * gain_inputs).astype(jnp.bfloat16)
        train_hidden = train_out_grads[layer_index].reshape(N_EX, ET_DEV, FFW)
        train_input = train_inputs[layer_index].reshape(N_EX, ET_DEV, D)
        scaled_hidden = (train_hidden * gain_hidden).astype(jnp.bfloat16)
        scaled_inputs = (train_input * gain_inputs).astype(jnp.bfloat16)

        def one_shard(items):
            part_hidden, part_input, part_scaled_h, part_scaled_a, part_hot = items
            cross = jnp.dot(rot_hidden, part_hidden.T, preferred_element_type=jnp.float32) * jnp.dot(rot_inputs, part_input.T, preferred_element_type=jnp.float32)
            scores = jnp.dot(jnp.dot(query_hot, cross, precision=lax.Precision.HIGHEST), part_hot.T, precision=lax.Precision.HIGHEST)
            own_pairs = jnp.dot(part_scaled_h, part_hidden.T, preferred_element_type=jnp.float32) * jnp.dot(part_scaled_a, part_input.T, preferred_element_type=jnp.float32)
            own_self = lax.optimization_barrier(jnp.sum(jnp.dot(part_hot, own_pairs, precision=lax.Precision.HIGHEST) * part_hot, axis=1))
            return (scores, own_self)
        shard_scores, shard_self = lax.map(one_shard, (train_hidden, train_input, scaled_hidden, scaled_inputs, example_hot))
        pair_scores = pair_scores + shard_scores
        self_influence = self_influence + shard_self
    relative = pair_scores / jnp.sqrt(self_influence + 1e-06)[:, None, :]
    return jnp.transpose(relative, (1, 0, 2)).reshape(QUERIES, EXAMPLES)
```

```python
import functools

import jax
import jax.numpy as jnp
from jax import lax
from jax.experimental import pallas as pl
from jax.experimental.pallas import tpu as pltpu
from jax.sharding import PartitionSpec as P

E_DEV = 2
QUERIES = 8
DAMP = 0.1
LANES = 128
MIB = 2**20
BY_LANES = (((1,), (1,)), ((), ()))


def vmem(x):
    return pltpu.with_memory_space_constraint(x, pltpu.VMEM)


def hbm(x):
    return pltpu.with_memory_space_constraint(x, pltpu.HBM)


def gather(x, shards):
    x = x[None]
    masks = [0]
    stride = shards
    while True:
        radix = min(4, stride // 2) if stride > 2 else stride
        stride //= radix
        parts, of_parts = [x], [masks]
        for m in reversed(range(1, radix)):
            mask = m * stride
            parts.append(lax.ppermute(x, "ex", [(i, i ^ mask) for i in range(shards)]))
            of_parts.append([mask ^ old for old in masks])
        if stride == 1:
            return parts, of_parts
        x = jnp.concatenate(parts, axis=0)
        masks = sum(of_parts, [])


def in_order(parts, masks):
    place = {mask: at for at, mask in enumerate(sum(masks, []))}
    device = jnp.bitwise_xor(jnp.arange(len(place), dtype=jnp.int32), lax.axis_index("ex"))
    table = jnp.array([place[mask] for mask in range(len(place))], dtype=jnp.int32)
    return jnp.concatenate(parts, axis=0)[table[device]]


def join_kernel(hidden, inputs, out, sems):
    width_h = hidden.shape[1]
    copies = [
        pltpu.make_async_copy(hidden, out.at[:, :width_h], sems.at[0]),
        pltpu.make_async_copy(inputs, out.at[:, width_h:], sems.at[1]),
    ]
    for copy in copies:
        copy.start()
    for copy in copies:
        copy.wait()


def self_kernel(train_h, train_i, eig_h, eig_i, ids, out):
    def pairs(train, eig):
        values = train[...]
        scaled = (values.astype(jnp.float32) * (1.0 / (eig[...] + DAMP))).astype(jnp.bfloat16)
        return lax.dot_general(scaled, values, BY_LANES, preferred_element_type=jnp.float32)

    own_pairs = pairs(train_h, eig_h) * pairs(train_i, eig_i)
    row = lax.broadcasted_iota(jnp.int32, (out.shape[0], ids.shape[1]), 0)
    hot = (ids[...] == row - E_DEV).astype(jnp.float32)
    sums = jnp.dot(
        hot, own_pairs, precision=lax.Precision.HIGHEST, preferred_element_type=jnp.float32
    )
    out[...] = jnp.broadcast_to(jnp.sum(sums * hot, axis=1, keepdims=True), out.shape)


def rotate_kernel(masks, *refs):
    parts = refs[:-6]
    basis_h, basis_i, eig_h, eig_i, out, tokens = refs[-6:]
    width_h = basis_h.shape[0]
    hid_block = basis_h.shape[1]
    inp_block = basis_i.shape[1]
    me = lax.axis_index("ex")
    own_tokens = parts[0].shape[1]
    rows = tokens.shape[0]
    column = lax.broadcasted_iota(jnp.int32, (rows, rows), 1)
    device_of = jnp.zeros((rows, rows), jnp.int32)
    at = 0
    for part, of_part in zip(parts, masks):
        for i, mask in enumerate(of_part):
            tokens[pl.ds(at, own_tokens), :] = part[i].astype(jnp.float32)
            device_of = jnp.where(column // own_tokens == at // own_tokens, me ^ mask, device_of)
            at += own_tokens
    token = lax.broadcasted_iota(jnp.int32, (rows, rows), 0)
    order = (token == device_of * own_tokens + column % own_tokens).astype(jnp.bfloat16)

    def rotate(lanes, basis, eig, block, to):
        product = jnp.dot(
            tokens[:, lanes].astype(jnp.bfloat16), basis[...], preferred_element_type=jnp.float32
        )
        at = pl.ds(pl.multiple_of(me * block, LANES), block)
        rotated = (product * (1.0 / (eig[:, at] + DAMP))).astype(jnp.bfloat16)
        out[0, :, to] = jnp.dot(order, rotated, preferred_element_type=jnp.float32).astype(
            jnp.bfloat16
        )

    rotate(slice(0, width_h), basis_h, eig_h, hid_block, slice(0, hid_block))
    rotate(slice(width_h, None), basis_i, eig_i, inp_block, slice(hid_block, None))


def score_kernel(masks, hid_block, inp_block, *refs):
    parts = refs[:-6]
    train_h, train_i, query_ids, ids, own_self, out = refs[-6:]
    me = lax.axis_index("ex")
    gram_h = gram_i = 0.0
    for part, of_part in zip(parts, masks):
        for i, mask in enumerate(of_part):
            block = me ^ mask
            at_h = pl.ds(pl.multiple_of(block * hid_block, LANES), hid_block)
            at_i = pl.ds(pl.multiple_of(block * inp_block, LANES), inp_block)
            gram_h += lax.dot_general(
                part[i, :, :hid_block],
                train_h[:, at_h],
                BY_LANES,
                preferred_element_type=jnp.float32,
            )
            gram_i += lax.dot_general(
                part[i, :, hid_block:],
                train_i[:, at_i],
                BY_LANES,
                preferred_element_type=jnp.float32,
            )
    row = lax.broadcasted_iota(jnp.int32, (out.shape[0], ids.shape[1]), 0)
    example_hot = ((ids[...] == row) & (row < E_DEV)).astype(jnp.float32)
    summed = lax.dot_general(
        example_hot,
        gram_h * gram_i,
        BY_LANES,
        precision=lax.Precision.HIGHEST,
        preferred_element_type=jnp.float32,
    )
    query = lax.broadcasted_iota(jnp.int32, (LANES, query_ids.shape[1]), 0)
    query_hot = (query_ids[...] == query).astype(jnp.float32)
    scores = lax.dot_general(
        summed,
        query_hot,
        BY_LANES,
        precision=lax.Precision.HIGHEST,
        preferred_element_type=jnp.float32,
    )
    out[...] = scores + own_self[...]


def finish_kernel(mine, other, out):
    total = mine[...] + other[...]
    half = QUERIES // 2
    relative = total[:E_DEV] / jnp.sqrt(total[E_DEV : 2 * E_DEV] + 1e-06)
    out[...] = jnp.where(
        lax.axis_index("layer") == 0, relative[:, :half], relative[:, half:QUERIES]
    )


def call(kernel, name, out_shape, flops=0, moved=0, **more):
    return pl.pallas_call(
        kernel,
        out_shape=out_shape,
        name=name,
        compiler_params=pltpu.CompilerParams(vmem_limit_bytes=8 * MIB),
        cost_estimate=pl.CostEstimate(flops=flops, bytes_accessed=moved, transcendentals=0),
        **more,
    )


def layer_swap(x):
    return lax.ppermute(x, "layer", [(0, 1), (1, 0)])


def body(
    query_out_grads,
    query_inputs,
    train_out_grads,
    train_inputs,
    basis_hidden,
    basis_inputs,
    eig_hidden,
    eig_inputs,
    query_ids,
    example_ids,
):
    shards = lax.axis_size("ex")
    hid_block = basis_hidden.shape[2]
    inp_block = basis_inputs.shape[2]
    rest = (
        train_out_grads[0],
        train_inputs[0],
        basis_hidden[0],
        basis_inputs[0],
        eig_hidden,
        eig_inputs,
        query_ids[None, :],
        example_ids,
    )
    if hid_block % LANES or inp_block % LANES:
        own = jnp.concatenate([query_out_grads[0], query_inputs[0]], axis=1)
        return plain(own, *rest)
    train_h, train_i, basis_h, basis_i, eig_h, eig_i, query_ids, example_ids = map(vmem, rest)
    own_tokens = query_inputs.shape[1]
    width = query_out_grads.shape[2] + query_inputs.shape[2]
    tokens = own_tokens * shards
    own = call(
        join_kernel,
        "join",
        pltpu.VMEM((own_tokens, width), jnp.bfloat16),
        flops=20_000_000_000,
        in_specs=[pl.BlockSpec(memory_space=pl.ANY)] * 2,
        out_specs=pl.BlockSpec(memory_space=pltpu.VMEM),
        scratch_shapes=[pltpu.SemaphoreType.DMA((2,))],
    )(hbm(query_out_grads[0]), hbm(query_inputs[0]))
    everyone, masks = gather(own, shards)
    small = jax.ShapeDtypeStruct((8, LANES), jnp.float32)
    own_self = call(
        self_kernel, "self_influence", small, flops=2 * 160 * 160 * 11264, moved=3_700_000
    )(train_h, train_i, eig_h, eig_i, example_ids)
    rotated = call(
        functools.partial(rotate_kernel, masks),
        "rotate",
        jax.ShapeDtypeStruct((1, tokens, hid_block + inp_block), jnp.bfloat16),
        flops=2 * 16 * 8_500_000,
        moved=17_000_000,
        scratch_shapes=[pltpu.VMEM((tokens, width), jnp.float32)],
    )(*everyone, basis_h, basis_i, eig_h, eig_i)
    parts, masks = gather(rotated[0], shards)
    mine = call(functools.partial(score_kernel, masks, hid_block, inp_block), "scores", small)(
        *parts, train_h, train_i, query_ids, example_ids, own_self
    )
    return call(
        finish_kernel,
        "finish",
        jax.ShapeDtypeStruct((E_DEV, QUERIES // 2), jnp.float32),
    )(mine, layer_swap(mine)).T


def plain(own, train_h, train_i, basis_h, basis_i, eig_h, eig_i, query_ids, example_ids):
    shards = lax.axis_size("ex")
    my_index = lax.axis_index("ex")
    width_h, hid_block = basis_h.shape
    inp_block = basis_i.shape[1]
    everyone = in_order(*gather(own, shards)).reshape(-1, own.shape[1])
    gain_h = 1.0 / (eig_h + DAMP)
    gain_i = 1.0 / (eig_i + DAMP)

    def rotate(tokens, basis, gain, block):
        product = jnp.dot(tokens, basis, preferred_element_type=jnp.float32)
        own_gain = lax.dynamic_slice_in_dim(gain, my_index * block, block, 1)
        return (product * own_gain).astype(jnp.bfloat16)

    rot_h = rotate(everyone[:, :width_h], basis_h, gain_h, hid_block)
    rot_i = rotate(everyone[:, width_h:], basis_i, gain_i, inp_block)
    pieces = in_order(*gather(jnp.concatenate([rot_h, rot_i], axis=1), shards))

    def gram(piece, train):
        split = train.reshape(train.shape[0], shards, -1)
        return jnp.einsum("nqf,tnf->qt", piece, split, preferred_element_type=jnp.float32)

    cross = gram(pieces[:, :, :hid_block], train_h) * gram(pieces[:, :, hid_block:], train_i)
    query_hot = query_ids == jnp.arange(QUERIES, dtype=jnp.int32)[:, None]
    example_hot = (example_ids == jnp.arange(E_DEV, dtype=jnp.int32)[:, None]).astype(jnp.float32)
    summed = jnp.dot(query_hot.astype(jnp.float32), cross, precision=lax.Precision.HIGHEST)
    scores = jnp.dot(summed, example_hot.T, precision=lax.Precision.HIGHEST)

    def pairs(train, gain):
        scaled = (train * gain).astype(jnp.bfloat16)
        return jnp.dot(scaled, train.T, preferred_element_type=jnp.float32)

    own_pairs = pairs(train_h, gain_h) * pairs(train_i, gain_i)
    sums = jnp.dot(example_hot, own_pairs, precision=lax.Precision.HIGHEST)
    own_self = jnp.sum(sums * example_hot, axis=1)
    mine = jnp.concatenate([scores, jnp.broadcast_to(own_self, scores.shape)], axis=1)
    total = mine + layer_swap(mine)
    half = QUERIES // 2
    total = lax.dynamic_slice_in_dim(total, lax.axis_index("layer") * half, half, 0)
    return total[:, :E_DEV] / jnp.sqrt(total[:, E_DEV:] + 1e-06)


def solution(mesh):
    in_specs = (
        P("layer", ("groups", "ex"), None),
        P("layer", ("groups", "ex"), None),
        P("layer", ("groups", "ex"), None),
        P("layer", ("groups", "ex"), None),
        P("layer", None, "ex"),
        P("layer", None, "ex"),
        P("layer", None),
        P("layer", None),
        P("groups"),
        P(("groups", "ex"), None),
    )
    out_specs = P(("groups", "layer"), "ex")
    return jax.shard_map(body, mesh=mesh, in_specs=in_specs, out_specs=out_specs, check_vma=False)
```

```python
import functools

import jax
import jax.numpy as jnp
from jax import lax
from jax.experimental import pallas as pl
from jax.experimental.pallas import tpu as pltpu
from jax.sharding import PartitionSpec as P

E_DEV = 2
QUERIES = 8
DAMP = 0.1
LANES = 128
MIB = 2**20
X, Z, FAR = 1, 2, 4
PLAN = [(Z, (0,)), (FAR, (0,)), (X ^ FAR, (0, Z)), (X, (0, Z)), (Z, (FAR,))]
BY_LANES = (((1,), (1,)), ((), ()))


def vmem(x):
    return pltpu.with_memory_space_constraint(x, pltpu.VMEM)


def hbm(x):
    return pltpu.with_memory_space_constraint(x, pltpu.HBM)


def steps(shards):
    if shards == 8:
        return PLAN
    plan, known, stride = [], [0], shards
    while stride > 1:
        radix = min(4, stride)
        stride //= radix
        plan += [(m * stride, tuple(known)) for m in range(1, radix)]
        known = [k ^ (m * stride) for m in range(radix) for k in known]
    return plan


def gather(x, shards):
    x = x[None]
    parts, masks = [x], [[0]]
    blocks, joined = {0: x}, {(0,): x}
    for mask, sent in steps(shards):
        if sent not in joined:
            joined[sent] = jnp.concatenate([blocks[s] for s in sent], axis=0)
        part = lax.ppermute(joined[sent], "ex", [(i, i ^ mask) for i in range(shards)])
        parts.append(part)
        masks.append([mask ^ s for s in sent])
        for i, s in enumerate(sent):
            blocks[mask ^ s] = part[i : i + 1]
    return parts, masks


def in_order(parts, masks):
    place = {mask: at for at, mask in enumerate(sum(masks, []))}
    device = jnp.bitwise_xor(jnp.arange(len(place), dtype=jnp.int32), lax.axis_index("ex"))
    table = jnp.array([place[mask] for mask in range(len(place))], dtype=jnp.int32)
    return jnp.concatenate(parts, axis=0)[table[device]]


def join_kernel(hidden, inputs, out, sems):
    width_h = hidden.shape[1]
    copies = [
        pltpu.make_async_copy(hidden, out.at[:, :width_h], sems.at[0]),
        pltpu.make_async_copy(inputs, out.at[:, width_h:], sems.at[1]),
    ]
    for copy in copies:
        copy.start()
    for copy in copies:
        copy.wait()


def self_kernel(train_h, train_i, eig_h, eig_i, ids, out):
    def pairs(train, eig):
        values = train[...]
        scaled = (values.astype(jnp.float32) * (1.0 / (eig[...] + DAMP))).astype(jnp.bfloat16)
        return lax.dot_general(scaled, values, BY_LANES, preferred_element_type=jnp.float32)

    own_pairs = pairs(train_h, eig_h) * pairs(train_i, eig_i)
    row = lax.broadcasted_iota(jnp.int32, (out.shape[0], ids.shape[1]), 0)
    hot = (ids[...] == row - E_DEV).astype(jnp.float32)
    sums = jnp.dot(
        hot, own_pairs, precision=lax.Precision.HIGHEST, preferred_element_type=jnp.float32
    )
    out[...] = jnp.broadcast_to(jnp.sum(sums * hot, axis=1, keepdims=True), out.shape)


def rotate_kernel(masks, *refs):
    parts = refs[:-7]
    basis_h, basis_i, eig_h, eig_i, _, out, tokens = refs[-7:]
    width_h = basis_h.shape[0]
    hid_block = basis_h.shape[1]
    inp_block = basis_i.shape[1]
    me = lax.axis_index("ex")
    own_tokens = parts[0].shape[1]
    rows = tokens.shape[0]
    column = lax.broadcasted_iota(jnp.int32, (rows, rows), 1)
    device_of = jnp.zeros((rows, rows), jnp.int32)
    at = 0
    for part, of_part in zip(parts, masks):
        for i, mask in enumerate(of_part):
            tokens[pl.ds(at, own_tokens), :] = part[i].astype(jnp.float32)
            device_of = jnp.where(column // own_tokens == at // own_tokens, me ^ mask, device_of)
            at += own_tokens
    token = lax.broadcasted_iota(jnp.int32, (rows, rows), 0)
    order = (token == device_of * own_tokens + column % own_tokens).astype(jnp.bfloat16)

    def rotate(lanes, basis, eig, block, to):
        product = jnp.dot(
            tokens[:, lanes].astype(jnp.bfloat16), basis[...], preferred_element_type=jnp.float32
        )
        at = pl.ds(pl.multiple_of(me * block, LANES), block)
        rotated = (product * (1.0 / (eig[:, at] + DAMP))).astype(jnp.bfloat16)
        out[0, :, to] = jnp.dot(order, rotated, preferred_element_type=jnp.float32).astype(
            jnp.bfloat16
        )

    rotate(slice(0, width_h), basis_h, eig_h, hid_block, slice(0, hid_block))
    rotate(slice(width_h, None), basis_i, eig_i, inp_block, slice(hid_block, None))


def add_grams(grams, masks, parts, train_h, train_i):
    me = lax.axis_index("ex")
    trains = (train_h, train_i)
    ends = [train.shape[1] // lax.axis_size("ex") for train in trains]
    lanes = (slice(0, ends[0]), slice(ends[0], None))
    for part, of_part in zip(parts, masks):
        for i, mask in enumerate(of_part):
            block = me ^ mask
            grams = [
                gram
                + lax.dot_general(
                    part[i, :, at],
                    train[:, pl.ds(pl.multiple_of(block * size, LANES), size)],
                    BY_LANES,
                    preferred_element_type=jnp.float32,
                )
                for gram, train, size, at in zip(grams, trains, ends, lanes)
            ]
    return grams


def early_kernel(masks, *refs):
    parts = refs[:-5]
    train_h, train_i, query_ids, grams, query_hot = refs[-5:]
    grams[0], grams[1] = add_grams((0.0, 0.0), masks, parts, train_h, train_i)
    tokens = query_ids.shape[1]
    row = lax.broadcasted_iota(jnp.int32, (tokens, tokens), 0)
    column = lax.broadcasted_iota(jnp.int32, (tokens, tokens), 1)
    own_id = jnp.where(row == column, jnp.broadcast_to(query_ids[...], (tokens, tokens)), 0)
    own_id = jnp.sum(own_id.astype(jnp.float32), axis=1, keepdims=True)
    query = lax.broadcasted_iota(jnp.int32, query_hot.shape, 1).astype(jnp.float32)
    query_hot[...] = (own_id == query).astype(jnp.float32)


def late_kernel(masks, *refs):
    parts = refs[:-7]
    train_h, train_i, grams, query_hot, ids, own_self, out = refs[-7:]
    gram_h, gram_i = add_grams((grams[0], grams[1]), masks, parts, train_h, train_i)
    cross = gram_h * gram_i
    row = lax.broadcasted_iota(jnp.int32, out.shape, 0)
    scores = own_self[...]
    for e in range(E_DEV):
        of_token = jnp.sum(jnp.where(ids[...] == e, cross, 0.0), axis=1, keepdims=True)
        of_query = jnp.sum(of_token * query_hot[...], axis=0, keepdims=True)
        scores = jnp.where(row == e, of_query, scores)
    out[...] = scores


def finish_kernel(mine, other, out):
    total = mine[...] + other[...]
    half = QUERIES // 2
    relative = total[:E_DEV] / jnp.sqrt(total[E_DEV : 2 * E_DEV] + 1e-06)
    out[...] = jnp.where(
        lax.axis_index("layer") == 0, relative[:, :half], relative[:, half:QUERIES]
    )


def call(kernel, name, out_shape, flops=0, moved=0, **more):
    return pl.pallas_call(
        kernel,
        out_shape=out_shape,
        name=name,
        compiler_params=pltpu.CompilerParams(vmem_limit_bytes=8 * MIB),
        cost_estimate=pl.CostEstimate(flops=flops, bytes_accessed=moved, transcendentals=0),
        **more,
    )


def layer_swap(x):
    return lax.ppermute(x, "layer", [(0, 1), (1, 0)])


def body(
    query_out_grads,
    query_inputs,
    train_out_grads,
    train_inputs,
    basis_hidden,
    basis_inputs,
    eig_hidden,
    eig_inputs,
    query_ids,
    example_ids,
):
    shards = lax.axis_size("ex")
    hid_block = basis_hidden.shape[2]
    inp_block = basis_inputs.shape[2]
    rest = (
        train_out_grads[0],
        train_inputs[0],
        basis_hidden[0],
        basis_inputs[0],
        eig_hidden,
        eig_inputs,
        query_ids[None, :],
        example_ids,
    )
    if hid_block % LANES or inp_block % LANES:
        own = jnp.concatenate([query_out_grads[0], query_inputs[0]], axis=1)
        return plain(own, *rest)
    train_h, train_i, basis_h, basis_i, eig_h, eig_i, query_ids, example_ids = map(vmem, rest)
    own_tokens = query_inputs.shape[1]
    width = query_out_grads.shape[2] + query_inputs.shape[2]
    tokens = own_tokens * shards
    own = call(
        join_kernel,
        "join",
        pltpu.VMEM((own_tokens, width), jnp.bfloat16),
        flops=20_000_000_000,
        in_specs=[pl.BlockSpec(memory_space=pl.ANY)] * 2,
        out_specs=pl.BlockSpec(memory_space=pltpu.VMEM),
        scratch_shapes=[pltpu.SemaphoreType.DMA((2,))],
    )(hbm(query_out_grads[0]), hbm(query_inputs[0]))
    everyone, masks = gather(own, shards)
    small = jax.ShapeDtypeStruct((8, LANES), jnp.float32)
    own_self = call(
        self_kernel, "self_influence", small, flops=2 * 160 * 160 * 11264, moved=3_700_000
    )(train_h, train_i, eig_h, eig_i, example_ids)
    rotated = call(
        functools.partial(rotate_kernel, masks),
        "rotate",
        jax.ShapeDtypeStruct((1, tokens, hid_block + inp_block), jnp.bfloat16),
        flops=2 * 16 * 8_500_000,
        moved=17_000_000,
        scratch_shapes=[pltpu.VMEM((tokens, width), jnp.float32)],
    )(*everyone, basis_h, basis_i, eig_h, eig_i, own_self)
    parts, masks = gather(rotated[0], shards)
    first = 3
    grams, query_hot = call(
        functools.partial(early_kernel, masks[:first]),
        "early_grams",
        (
            jax.ShapeDtypeStruct((2, tokens, train_h.shape[0]), jnp.float32),
            jax.ShapeDtypeStruct((tokens, LANES), jnp.float32),
        ),
        flops=500_000_000,
    )(*parts[:first], train_h, train_i, query_ids)
    mine = call(functools.partial(late_kernel, masks[first:]), "scores", small)(
        *parts[first:], train_h, train_i, grams, query_hot, example_ids, own_self
    )
    return call(
        finish_kernel,
        "finish",
        jax.ShapeDtypeStruct((E_DEV, QUERIES // 2), jnp.float32),
    )(mine, layer_swap(mine)).T


def plain(own, train_h, train_i, basis_h, basis_i, eig_h, eig_i, query_ids, example_ids):
    shards = lax.axis_size("ex")
    my_index = lax.axis_index("ex")
    width_h, hid_block = basis_h.shape
    inp_block = basis_i.shape[1]
    everyone = in_order(*gather(own, shards)).reshape(-1, own.shape[1])
    gain_h = 1.0 / (eig_h + DAMP)
    gain_i = 1.0 / (eig_i + DAMP)

    def rotate(tokens, basis, gain, block):
        product = jnp.dot(tokens, basis, preferred_element_type=jnp.float32)
        own_gain = lax.dynamic_slice_in_dim(gain, my_index * block, block, 1)
        return (product * own_gain).astype(jnp.bfloat16)

    rot_h = rotate(everyone[:, :width_h], basis_h, gain_h, hid_block)
    rot_i = rotate(everyone[:, width_h:], basis_i, gain_i, inp_block)
    pieces = in_order(*gather(jnp.concatenate([rot_h, rot_i], axis=1), shards))

    def gram(piece, train):
        split = train.reshape(train.shape[0], shards, -1)
        return jnp.einsum("nqf,tnf->qt", piece, split, preferred_element_type=jnp.float32)

    cross = gram(pieces[:, :, :hid_block], train_h) * gram(pieces[:, :, hid_block:], train_i)
    query_hot = query_ids == jnp.arange(QUERIES, dtype=jnp.int32)[:, None]
    example_hot = (example_ids == jnp.arange(E_DEV, dtype=jnp.int32)[:, None]).astype(jnp.float32)
    summed = jnp.dot(query_hot.astype(jnp.float32), cross, precision=lax.Precision.HIGHEST)
    scores = jnp.dot(summed, example_hot.T, precision=lax.Precision.HIGHEST)

    def pairs(train, gain):
        scaled = (train * gain).astype(jnp.bfloat16)
        return jnp.dot(scaled, train.T, preferred_element_type=jnp.float32)

    own_pairs = pairs(train_h, gain_h) * pairs(train_i, gain_i)
    sums = jnp.dot(example_hot, own_pairs, precision=lax.Precision.HIGHEST)
    own_self = jnp.sum(sums * example_hot, axis=1)
    mine = jnp.concatenate([scores, jnp.broadcast_to(own_self, scores.shape)], axis=1)
    total = mine + layer_swap(mine)
    half = QUERIES // 2
    total = lax.dynamic_slice_in_dim(total, lax.axis_index("layer") * half, half, 0)
    return total[:, :E_DEV] / jnp.sqrt(total[:, E_DEV:] + 1e-06)


def solution(mesh):
    in_specs = (
        P("layer", ("groups", "ex"), None),
        P("layer", ("groups", "ex"), None),
        P("layer", ("groups", "ex"), None),
        P("layer", ("groups", "ex"), None),
        P("layer", None, "ex"),
        P("layer", None, "ex"),
        P("layer", None),
        P("layer", None),
        P("groups"),
        P(("groups", "ex"), None),
    )
    out_specs = P(("groups", "layer"), "ex")
    return jax.shard_map(body, mesh=mesh, in_specs=in_specs, out_specs=out_specs, check_vma=False)
```

```python
import functools

import jax
import jax.numpy as jnp
from jax import lax
from jax.experimental import pallas as pl
from jax.experimental.pallas import tpu as pltpu
from jax.sharding import PartitionSpec as P

E_DEV = 2
QUERIES = 8
DAMP = 0.1
LANES = 128
MIB = 2**20
X, Z, FAR = 1, 2, 4
PLAN = [(X, (0,)), (FAR, (0,)), (Z ^ FAR, (0, X)), (Z, (0, X)), (X, (FAR,))]
BY_LANES = (((1,), (1,)), ((), ()))


def vmem(x):
    return pltpu.with_memory_space_constraint(x, pltpu.VMEM)


def hbm(x):
    return pltpu.with_memory_space_constraint(x, pltpu.HBM)


def steps(shards):
    if shards == 8:
        return PLAN
    plan, known, stride = [], [0], shards
    while stride > 1:
        radix = min(4, stride)
        stride //= radix
        plan += [(m * stride, tuple(known)) for m in range(1, radix)]
        known = [k ^ (m * stride) for m in range(radix) for k in known]
    return plan


def gather(x, shards):
    x = x[None]
    parts, masks = [x], [[0]]
    blocks, joined = {0: x}, {(0,): x}
    for mask, sent in steps(shards):
        if sent not in joined:
            joined[sent] = jnp.concatenate([blocks[s] for s in sent], axis=0)
        part = lax.ppermute(joined[sent], "ex", [(i, i ^ mask) for i in range(shards)])
        parts.append(part)
        masks.append([mask ^ s for s in sent])
        for i, s in enumerate(sent):
            blocks[mask ^ s] = part[i : i + 1]
    return parts, masks


def in_order(parts, masks):
    place = {mask: at for at, mask in enumerate(sum(masks, []))}
    device = jnp.bitwise_xor(jnp.arange(len(place), dtype=jnp.int32), lax.axis_index("ex"))
    table = jnp.array([place[mask] for mask in range(len(place))], dtype=jnp.int32)
    return jnp.concatenate(parts, axis=0)[table[device]]


def join_kernel(hidden, inputs, out, sems):
    width_h = hidden.shape[1]
    copies = [
        pltpu.make_async_copy(hidden, out.at[:, :width_h], sems.at[0]),
        pltpu.make_async_copy(inputs, out.at[:, width_h:], sems.at[1]),
    ]
    for copy in copies:
        copy.start()
    for copy in copies:
        copy.wait()


def self_kernel(train_h, train_i, eig_h, eig_i, ids, out):
    def pairs(train, eig):
        values = train[...]
        scaled = (values.astype(jnp.float32) * (1.0 / (eig[...] + DAMP))).astype(jnp.bfloat16)
        return lax.dot_general(scaled, values, BY_LANES, preferred_element_type=jnp.float32)

    own_pairs = pairs(train_h, eig_h) * pairs(train_i, eig_i)
    row = lax.broadcasted_iota(jnp.int32, (out.shape[0], ids.shape[1]), 0)
    hot = (ids[...] == row - E_DEV).astype(jnp.float32)
    sums = jnp.dot(
        hot, own_pairs, precision=lax.Precision.HIGHEST, preferred_element_type=jnp.float32
    )
    out[...] = jnp.broadcast_to(jnp.sum(sums * hot, axis=1, keepdims=True), out.shape)


def rotate_kernel(masks, *refs):
    parts = refs[:-7]
    basis_h, basis_i, eig_h, eig_i, _, out, tokens = refs[-7:]
    width_h = basis_h.shape[0]
    hid_block = basis_h.shape[1]
    inp_block = basis_i.shape[1]
    me = lax.axis_index("ex")
    for part, of_part in zip(parts, masks):
        for i, mask in enumerate(of_part):
            tokens[me ^ mask] = part[i]

    def rotate(lanes, basis, eig, block, to):
        in_order = jnp.concatenate([tokens[k, :, lanes] for k in range(tokens.shape[0])], axis=0)
        product = jnp.dot(in_order, basis[...], preferred_element_type=jnp.float32)
        at = pl.ds(pl.multiple_of(me * block, LANES), block)
        out[0, :, to] = (product * (1.0 / (eig[:, at] + DAMP))).astype(jnp.bfloat16)

    rotate(slice(0, width_h), basis_h, eig_h, hid_block, slice(0, hid_block))
    rotate(slice(width_h, None), basis_i, eig_i, inp_block, slice(hid_block, None))


def add_grams(grams, masks, parts, train_h, train_i):
    me = lax.axis_index("ex")
    trains = (train_h, train_i)
    ends = [train.shape[1] // lax.axis_size("ex") for train in trains]
    lanes = (slice(0, ends[0]), slice(ends[0], None))
    for part, of_part in zip(parts, masks):
        for i, mask in enumerate(of_part):
            block = me ^ mask
            grams = [
                gram
                + lax.dot_general(
                    part[i, :, at],
                    train[:, pl.ds(pl.multiple_of(block * size, LANES), size)],
                    BY_LANES,
                    preferred_element_type=jnp.float32,
                )
                for gram, train, size, at in zip(grams, trains, ends, lanes)
            ]
    return grams


def early_kernel(masks, *refs):
    parts = refs[:-5]
    train_h, train_i, query_ids, grams, query_hot = refs[-5:]
    grams[0], grams[1] = add_grams((0.0, 0.0), masks, parts, train_h, train_i)
    tokens = query_ids.shape[1]
    row = lax.broadcasted_iota(jnp.int32, (tokens, tokens), 0)
    column = lax.broadcasted_iota(jnp.int32, (tokens, tokens), 1)
    own_id = jnp.where(row == column, jnp.broadcast_to(query_ids[...], (tokens, tokens)), 0)
    own_id = jnp.sum(own_id.astype(jnp.float32), axis=1, keepdims=True)
    query = lax.broadcasted_iota(jnp.int32, query_hot.shape, 1).astype(jnp.float32)
    query_hot[...] = (own_id == query).astype(jnp.float32)


def late_kernel(masks, *refs):
    parts = refs[:-7]
    train_h, train_i, grams, query_hot, ids, own_self, out = refs[-7:]
    gram_h, gram_i = add_grams((grams[0], grams[1]), masks, parts, train_h, train_i)
    cross = gram_h * gram_i
    row = lax.broadcasted_iota(jnp.int32, out.shape, 0)
    scores = own_self[...]
    for e in range(E_DEV):
        of_token = jnp.sum(jnp.where(ids[...] == e, cross, 0.0), axis=1, keepdims=True)
        of_query = jnp.sum(of_token * query_hot[...], axis=0, keepdims=True)
        scores = jnp.where(row == e, of_query, scores)
    out[...] = scores


def finish_kernel(mine, other, out):
    total = mine[...] + other[...]
    half = QUERIES // 2
    relative = total[:E_DEV] / jnp.sqrt(total[E_DEV : 2 * E_DEV] + 1e-06)
    out[...] = jnp.where(
        lax.axis_index("layer") == 0, relative[:, :half], relative[:, half:QUERIES]
    )


def call(kernel, name, out_shape, flops=0, moved=0, **more):
    return pl.pallas_call(
        kernel,
        out_shape=out_shape,
        name=name,
        compiler_params=pltpu.CompilerParams(vmem_limit_bytes=8 * MIB),
        cost_estimate=pl.CostEstimate(flops=flops, bytes_accessed=moved, transcendentals=0),
        **more,
    )


def layer_swap(x):
    return lax.ppermute(x, "layer", [(0, 1), (1, 0)])


def body(
    query_out_grads,
    query_inputs,
    train_out_grads,
    train_inputs,
    basis_hidden,
    basis_inputs,
    eig_hidden,
    eig_inputs,
    query_ids,
    example_ids,
):
    shards = lax.axis_size("ex")
    hid_block = basis_hidden.shape[2]
    inp_block = basis_inputs.shape[2]
    rest = (
        train_out_grads[0],
        train_inputs[0],
        basis_hidden[0],
        basis_inputs[0],
        eig_hidden,
        eig_inputs,
        query_ids[None, :],
        example_ids,
    )
    if hid_block % LANES or inp_block % LANES:
        own = jnp.concatenate([query_out_grads[0], query_inputs[0]], axis=1)
        return plain(own, *rest)
    train_h, train_i, basis_h, basis_i, eig_h, eig_i, query_ids, example_ids = map(vmem, rest)
    own_tokens = query_inputs.shape[1]
    width = query_out_grads.shape[2] + query_inputs.shape[2]
    tokens = own_tokens * shards
    own = call(
        join_kernel,
        "join",
        pltpu.VMEM((own_tokens, width), jnp.bfloat16),
        flops=20_000_000_000,
        in_specs=[pl.BlockSpec(memory_space=pl.ANY)] * 2,
        out_specs=pl.BlockSpec(memory_space=pltpu.VMEM),
        scratch_shapes=[pltpu.SemaphoreType.DMA((2,))],
    )(hbm(query_out_grads[0]), hbm(query_inputs[0]))
    everyone, masks = gather(own, shards)
    small = jax.ShapeDtypeStruct((8, LANES), jnp.float32)
    own_self = call(
        self_kernel, "self_influence", small, flops=2 * 160 * 160 * 11264, moved=3_700_000
    )(train_h, train_i, eig_h, eig_i, example_ids)
    rotated = call(
        functools.partial(rotate_kernel, masks),
        "rotate",
        jax.ShapeDtypeStruct((1, tokens, hid_block + inp_block), jnp.bfloat16),
        flops=2 * 16 * 8_500_000,
        moved=17_000_000,
        scratch_shapes=[pltpu.VMEM((shards, own_tokens, width), jnp.bfloat16)],
    )(*everyone, basis_h, basis_i, eig_h, eig_i, own_self)
    parts, masks = gather(rotated[0], shards)
    first = 3
    grams, query_hot = call(
        functools.partial(early_kernel, masks[:first]),
        "early_grams",
        (
            jax.ShapeDtypeStruct((2, tokens, train_h.shape[0]), jnp.float32),
            jax.ShapeDtypeStruct((tokens, LANES), jnp.float32),
        ),
        flops=500_000_000,
    )(*parts[:first], train_h, train_i, query_ids)
    mine = call(functools.partial(late_kernel, masks[first:]), "scores", small)(
        *parts[first:], train_h, train_i, grams, query_hot, example_ids, own_self
    )
    return call(
        finish_kernel,
        "finish",
        jax.ShapeDtypeStruct((E_DEV, QUERIES // 2), jnp.float32),
    )(mine, layer_swap(mine)).T


def plain(own, train_h, train_i, basis_h, basis_i, eig_h, eig_i, query_ids, example_ids):
    shards = lax.axis_size("ex")
    my_index = lax.axis_index("ex")
    width_h, hid_block = basis_h.shape
    inp_block = basis_i.shape[1]
    everyone = in_order(*gather(own, shards)).reshape(-1, own.shape[1])
    gain_h = 1.0 / (eig_h + DAMP)
    gain_i = 1.0 / (eig_i + DAMP)

    def rotate(tokens, basis, gain, block):
        product = jnp.dot(tokens, basis, preferred_element_type=jnp.float32)
        own_gain = lax.dynamic_slice_in_dim(gain, my_index * block, block, 1)
        return (product * own_gain).astype(jnp.bfloat16)

    rot_h = rotate(everyone[:, :width_h], basis_h, gain_h, hid_block)
    rot_i = rotate(everyone[:, width_h:], basis_i, gain_i, inp_block)
    pieces = in_order(*gather(jnp.concatenate([rot_h, rot_i], axis=1), shards))

    def gram(piece, train):
        split = train.reshape(train.shape[0], shards, -1)
        return jnp.einsum("nqf,tnf->qt", piece, split, preferred_element_type=jnp.float32)

    cross = gram(pieces[:, :, :hid_block], train_h) * gram(pieces[:, :, hid_block:], train_i)
    query_hot = query_ids == jnp.arange(QUERIES, dtype=jnp.int32)[:, None]
    example_hot = (example_ids == jnp.arange(E_DEV, dtype=jnp.int32)[:, None]).astype(jnp.float32)
    summed = jnp.dot(query_hot.astype(jnp.float32), cross, precision=lax.Precision.HIGHEST)
    scores = jnp.dot(summed, example_hot.T, precision=lax.Precision.HIGHEST)

    def pairs(train, gain):
        scaled = (train * gain).astype(jnp.bfloat16)
        return jnp.dot(scaled, train.T, preferred_element_type=jnp.float32)

    own_pairs = pairs(train_h, gain_h) * pairs(train_i, gain_i)
    sums = jnp.dot(example_hot, own_pairs, precision=lax.Precision.HIGHEST)
    own_self = jnp.sum(sums * example_hot, axis=1)
    mine = jnp.concatenate([scores, jnp.broadcast_to(own_self, scores.shape)], axis=1)
    total = mine + layer_swap(mine)
    half = QUERIES // 2
    total = lax.dynamic_slice_in_dim(total, lax.axis_index("layer") * half, half, 0)
    return total[:, :E_DEV] / jnp.sqrt(total[:, E_DEV:] + 1e-06)


def solution(mesh):
    in_specs = (
        P("layer", ("groups", "ex"), None),
        P("layer", ("groups", "ex"), None),
        P("layer", ("groups", "ex"), None),
        P("layer", ("groups", "ex"), None),
        P("layer", None, "ex"),
        P("layer", None, "ex"),
        P("layer", None),
        P("layer", None),
        P("groups"),
        P(("groups", "ex"), None),
    )
    out_specs = P(("groups", "layer"), "ex")
    return jax.shard_map(body, mesh=mesh, in_specs=in_specs, out_specs=out_specs, check_vma=False)
```

```python
import functools

import jax
import jax.numpy as jnp
from jax import lax
from jax.experimental import pallas as pl
from jax.experimental.pallas import tpu as pltpu
from jax.sharding import PartitionSpec as P

E_DEV = 2
QUERIES = 8
DAMP = 0.1
LANES = 128
MIB = 2**20
X, Z, FAR = 1, 2, 4
PLAN = [(X, (0,)), (FAR, (0,)), (Z ^ FAR, (0, X)), (Z, (0, X)), (X, (FAR,))]
BY_LANES = (((1,), (1,)), ((), ()))


def vmem(x):
    return pltpu.with_memory_space_constraint(x, pltpu.VMEM)


def hbm(x):
    return pltpu.with_memory_space_constraint(x, pltpu.HBM)


def steps(shards):
    if shards == 8:
        return PLAN
    plan, known, stride = [], [0], shards
    while stride > 1:
        radix = min(4, stride)
        stride //= radix
        plan += [(m * stride, tuple(known)) for m in range(1, radix)]
        known = [k ^ (m * stride) for m in range(radix) for k in known]
    return plan


def gather(x, shards):
    x = x[None]
    parts, masks = [x], [[0]]
    blocks, joined = {0: x}, {(0,): x}
    for mask, sent in steps(shards):
        if sent not in joined:
            joined[sent] = jnp.concatenate([blocks[s] for s in sent], axis=0)
        part = lax.ppermute(joined[sent], "ex", [(i, i ^ mask) for i in range(shards)])
        parts.append(part)
        masks.append([mask ^ s for s in sent])
        for i, s in enumerate(sent):
            blocks[mask ^ s] = part[i : i + 1]
    return parts, masks


def in_order(parts, masks):
    place = {mask: at for at, mask in enumerate(sum(masks, []))}
    device = jnp.bitwise_xor(jnp.arange(len(place), dtype=jnp.int32), lax.axis_index("ex"))
    table = jnp.array([place[mask] for mask in range(len(place))], dtype=jnp.int32)
    return jnp.concatenate(parts, axis=0)[table[device]]


def join_kernel(hidden, inputs, out, sems):
    width_h = hidden.shape[1]
    copies = [
        pltpu.make_async_copy(hidden, out.at[:, :width_h], sems.at[0]),
        pltpu.make_async_copy(inputs, out.at[:, width_h:], sems.at[1]),
    ]
    for copy in copies:
        copy.start()
    for copy in copies:
        copy.wait()


def self_kernel(train_h, train_i, eig_h, eig_i, ids, out):
    def pairs(train, eig):
        values = train[...]
        scaled = (values.astype(jnp.float32) * (1.0 / (eig[...] + DAMP))).astype(jnp.bfloat16)
        return lax.dot_general(scaled, values, BY_LANES, preferred_element_type=jnp.float32)

    own_pairs = pairs(train_h, eig_h) * pairs(train_i, eig_i)
    row = lax.broadcasted_iota(jnp.int32, (out.shape[0], ids.shape[1]), 0)
    hot = (ids[...] == row - E_DEV).astype(jnp.float32)
    sums = jnp.dot(
        hot, own_pairs, precision=lax.Precision.HIGHEST, preferred_element_type=jnp.float32
    )
    out[...] = jnp.broadcast_to(jnp.sum(sums * hot, axis=1, keepdims=True), out.shape)


def rotate_kernel(masks, *refs):
    parts = refs[:-7]
    basis_h, basis_i, eig_h, eig_i, _, out, tokens = refs[-7:]
    width_h = basis_h.shape[0]
    hid_block = basis_h.shape[1]
    inp_block = basis_i.shape[1]
    me = lax.axis_index("ex")
    for part, of_part in zip(parts, masks):
        for i, mask in enumerate(of_part):
            tokens[me ^ mask] = part[i]

    def rotate(lanes, basis, eig, block, to):
        in_order = jnp.concatenate([tokens[k, :, lanes] for k in range(tokens.shape[0])], axis=0)
        product = jnp.dot(in_order, basis[...], preferred_element_type=jnp.float32)
        at = pl.ds(pl.multiple_of(me * block, LANES), block)
        out[0, :, to] = (product * (1.0 / (eig[:, at] + DAMP))).astype(jnp.bfloat16)

    rotate(slice(0, width_h), basis_h, eig_h, hid_block, slice(0, hid_block))
    rotate(slice(width_h, None), basis_i, eig_i, inp_block, slice(hid_block, None))


def add_grams(grams, masks, parts, train_h, train_i):
    me = lax.axis_index("ex")
    trains = (train_h, train_i)
    ends = [train.shape[1] // lax.axis_size("ex") for train in trains]
    lanes = (slice(0, ends[0]), slice(ends[0], None))
    for part, of_part in zip(parts, masks):
        for i, mask in enumerate(of_part):
            block = me ^ mask
            grams = [
                gram
                + lax.dot_general(
                    part[i, :, at],
                    train[:, pl.ds(pl.multiple_of(block * size, LANES), size)],
                    BY_LANES,
                    preferred_element_type=jnp.float32,
                )
                for gram, train, size, at in zip(grams, trains, ends, lanes)
            ]
    return grams


def early_kernel(masks, *refs):
    parts = refs[:-5]
    train_h, train_i, query_ids, grams, query_hot = refs[-5:]
    grams[0], grams[1] = add_grams((0.0, 0.0), masks, parts, train_h, train_i)
    tokens = query_ids.shape[1]
    row = lax.broadcasted_iota(jnp.int32, (tokens, tokens), 0)
    column = lax.broadcasted_iota(jnp.int32, (tokens, tokens), 1)
    own_id = jnp.where(row == column, jnp.broadcast_to(query_ids[...], (tokens, tokens)), 0)
    own_id = jnp.sum(own_id.astype(jnp.float32), axis=1, keepdims=True)
    query = lax.broadcasted_iota(jnp.int32, query_hot.shape, 1).astype(jnp.float32)
    query_hot[...] = (own_id == query).astype(jnp.float32)


def more_kernel(masks, *refs):
    parts = refs[:-4]
    train_h, train_i, grams, out = refs[-4:]
    out[0], out[1] = add_grams((grams[0], grams[1]), masks, parts, train_h, train_i)


def late_kernel(masks, *refs):
    parts = refs[:-7]
    train_h, train_i, grams, query_hot, ids, own_self, out = refs[-7:]
    gram_h, gram_i = add_grams((grams[0], grams[1]), masks, parts, train_h, train_i)
    cross = gram_h * gram_i
    row = lax.broadcasted_iota(jnp.int32, out.shape, 0)
    scores = own_self[...]
    for e in range(E_DEV):
        of_token = jnp.sum(jnp.where(ids[...] == e, cross, 0.0), axis=1, keepdims=True)
        of_query = jnp.sum(of_token * query_hot[...], axis=0, keepdims=True)
        scores = jnp.where(row == e, of_query, scores)
    out[...] = scores


def finish_kernel(mine, other, out):
    total = mine[...] + other[...]
    half = QUERIES // 2
    relative = total[:E_DEV] / jnp.sqrt(total[E_DEV : 2 * E_DEV] + 1e-06)
    out[...] = jnp.where(
        lax.axis_index("layer") == 0, relative[:, :half], relative[:, half:QUERIES]
    )


def call(kernel, name, out_shape, flops=0, moved=0, **more):
    return pl.pallas_call(
        kernel,
        out_shape=out_shape,
        name=name,
        compiler_params=pltpu.CompilerParams(vmem_limit_bytes=8 * MIB),
        cost_estimate=pl.CostEstimate(flops=flops, bytes_accessed=moved, transcendentals=0),
        **more,
    )


def layer_swap(x):
    return lax.ppermute(x, "layer", [(0, 1), (1, 0)])


def body(
    query_out_grads,
    query_inputs,
    train_out_grads,
    train_inputs,
    basis_hidden,
    basis_inputs,
    eig_hidden,
    eig_inputs,
    query_ids,
    example_ids,
):
    shards = lax.axis_size("ex")
    hid_block = basis_hidden.shape[2]
    inp_block = basis_inputs.shape[2]
    rest = (
        train_out_grads[0],
        train_inputs[0],
        basis_hidden[0],
        basis_inputs[0],
        eig_hidden,
        eig_inputs,
        query_ids[None, :],
        example_ids,
    )
    if hid_block % LANES or inp_block % LANES:
        own = jnp.concatenate([query_out_grads[0], query_inputs[0]], axis=1)
        return plain(own, *rest)
    train_h, train_i, basis_h, basis_i, eig_h, eig_i, query_ids, example_ids = map(vmem, rest)
    own_tokens = query_inputs.shape[1]
    width = query_out_grads.shape[2] + query_inputs.shape[2]
    tokens = own_tokens * shards
    own = call(
        join_kernel,
        "join",
        pltpu.VMEM((own_tokens, width), jnp.bfloat16),
        flops=20_000_000_000,
        in_specs=[pl.BlockSpec(memory_space=pl.ANY)] * 2,
        out_specs=pl.BlockSpec(memory_space=pltpu.VMEM),
        scratch_shapes=[pltpu.SemaphoreType.DMA((2,))],
    )(hbm(query_out_grads[0]), hbm(query_inputs[0]))
    everyone, masks = gather(own, shards)
    small = jax.ShapeDtypeStruct((8, LANES), jnp.float32)
    own_self = call(
        self_kernel, "self_influence", small, flops=2 * 160 * 160 * 11264, moved=3_700_000
    )(train_h, train_i, eig_h, eig_i, example_ids)
    rotated = call(
        functools.partial(rotate_kernel, masks),
        "rotate",
        jax.ShapeDtypeStruct((1, tokens, hid_block + inp_block), jnp.bfloat16),
        flops=2 * 16 * 8_500_000,
        moved=17_000_000,
        scratch_shapes=[pltpu.VMEM((shards, own_tokens, width), jnp.bfloat16)],
    )(*everyone, basis_h, basis_i, eig_h, eig_i, own_self)
    parts, masks = gather(rotated[0], shards)
    gram_shape = jax.ShapeDtypeStruct((2, tokens, train_h.shape[0]), jnp.float32)
    first, last = 3, 4
    grams, query_hot = call(
        functools.partial(early_kernel, masks[:first]),
        "early_grams",
        (gram_shape, jax.ShapeDtypeStruct((tokens, LANES), jnp.float32)),
        flops=500_000_000,
    )(*parts[:first], train_h, train_i, query_ids)
    grams = call(functools.partial(more_kernel, masks[first:last]), "more_grams", gram_shape, flops=300_000_000)(
        *parts[first:last], train_h, train_i, grams
    )
    mine = call(functools.partial(late_kernel, masks[last:]), "scores", small)(
        *parts[last:], train_h, train_i, grams, query_hot, example_ids, own_self
    )
    return call(
        finish_kernel,
        "finish",
        jax.ShapeDtypeStruct((E_DEV, QUERIES // 2), jnp.float32),
    )(mine, layer_swap(mine)).T


def plain(own, train_h, train_i, basis_h, basis_i, eig_h, eig_i, query_ids, example_ids):
    shards = lax.axis_size("ex")
    my_index = lax.axis_index("ex")
    width_h, hid_block = basis_h.shape
    inp_block = basis_i.shape[1]
    everyone = in_order(*gather(own, shards)).reshape(-1, own.shape[1])
    gain_h = 1.0 / (eig_h + DAMP)
    gain_i = 1.0 / (eig_i + DAMP)

    def rotate(tokens, basis, gain, block):
        product = jnp.dot(tokens, basis, preferred_element_type=jnp.float32)
        own_gain = lax.dynamic_slice_in_dim(gain, my_index * block, block, 1)
        return (product * own_gain).astype(jnp.bfloat16)

    rot_h = rotate(everyone[:, :width_h], basis_h, gain_h, hid_block)
    rot_i = rotate(everyone[:, width_h:], basis_i, gain_i, inp_block)
    pieces = in_order(*gather(jnp.concatenate([rot_h, rot_i], axis=1), shards))

    def gram(piece, train):
        split = train.reshape(train.shape[0], shards, -1)
        return jnp.einsum("nqf,tnf->qt", piece, split, preferred_element_type=jnp.float32)

    cross = gram(pieces[:, :, :hid_block], train_h) * gram(pieces[:, :, hid_block:], train_i)
    query_hot = query_ids == jnp.arange(QUERIES, dtype=jnp.int32)[:, None]
    example_hot = (example_ids == jnp.arange(E_DEV, dtype=jnp.int32)[:, None]).astype(jnp.float32)
    summed = jnp.dot(query_hot.astype(jnp.float32), cross, precision=lax.Precision.HIGHEST)
    scores = jnp.dot(summed, example_hot.T, precision=lax.Precision.HIGHEST)

    def pairs(train, gain):
        scaled = (train * gain).astype(jnp.bfloat16)
        return jnp.dot(scaled, train.T, preferred_element_type=jnp.float32)

    own_pairs = pairs(train_h, gain_h) * pairs(train_i, gain_i)
    sums = jnp.dot(example_hot, own_pairs, precision=lax.Precision.HIGHEST)
    own_self = jnp.sum(sums * example_hot, axis=1)
    mine = jnp.concatenate([scores, jnp.broadcast_to(own_self, scores.shape)], axis=1)
    total = mine + layer_swap(mine)
    half = QUERIES // 2
    total = lax.dynamic_slice_in_dim(total, lax.axis_index("layer") * half, half, 0)
    return total[:, :E_DEV] / jnp.sqrt(total[:, E_DEV:] + 1e-06)


def solution(mesh):
    in_specs = (
        P("layer", ("groups", "ex"), None),
        P("layer", ("groups", "ex"), None),
        P("layer", ("groups", "ex"), None),
        P("layer", ("groups", "ex"), None),
        P("layer", None, "ex"),
        P("layer", None, "ex"),
        P("layer", None),
        P("layer", None),
        P("groups"),
        P(("groups", "ex"), None),
    )
    out_specs = P(("groups", "layer"), "ex")
    return jax.shard_map(body, mesh=mesh, in_specs=in_specs, out_specs=out_specs, check_vma=False)
```

```python
import functools

import jax
import jax.numpy as jnp
from jax import lax
from jax.experimental import pallas as pl
from jax.experimental.pallas import tpu as pltpu
from jax.sharding import PartitionSpec as P

E_DEV = 2
QUERIES = 8
DAMP = 0.1
LANES = 128
MIB = 2**20
X, Z, FAR = 1, 2, 4
QUERY_PLAN = [(FAR, (0,)), (X, (0,)), (Z, (0, X)), (Z ^ FAR, (0, X)), (X, (FAR,))]
ROTATED_PLAN = [(FAR, (0,)), (X, (0,)), (Z ^ FAR, (0, X)), (Z, (0, X)), (X, (FAR,))]
BY_LANES = (((1,), (1,)), ((), ()))


def vmem(x):
    return pltpu.with_memory_space_constraint(x, pltpu.VMEM)


def hbm(x):
    return pltpu.with_memory_space_constraint(x, pltpu.HBM)


def steps(shards, plan):
    if shards == 8:
        return plan
    plan, known, stride = [], [0], shards
    while stride > 1:
        radix = min(4, stride)
        stride //= radix
        plan += [(m * stride, tuple(known)) for m in range(1, radix)]
        known = [k ^ (m * stride) for m in range(radix) for k in known]
    return plan


def gather(x, shards, plan=QUERY_PLAN, by_kernel=False):
    x = x[None]
    parts, masks = [x], [[0]]
    blocks, joined = {0: x}, {(0,): x}
    for mask, sent in steps(shards, plan):
        if sent not in joined:
            if by_kernel and len(sent) == 2:
                joined[sent] = call(
                    pair_kernel, "pair", jax.ShapeDtypeStruct((2, *x.shape[1:]), x.dtype)
                )(*[blocks[s] for s in sent])
            else:
                joined[sent] = jnp.concatenate([blocks[s] for s in sent], axis=0)
        part = lax.ppermute(joined[sent], "ex", [(i, i ^ mask) for i in range(shards)])
        parts.append(part)
        masks.append([mask ^ s for s in sent])
        for i, s in enumerate(sent):
            blocks[mask ^ s] = part[i : i + 1]
    return parts, masks


def pair_kernel(first, second, out):
    out[:1] = first[...]
    out[1:] = second[...]


def in_order(parts, masks):
    place = {mask: at for at, mask in enumerate(sum(masks, []))}
    device = jnp.bitwise_xor(jnp.arange(len(place), dtype=jnp.int32), lax.axis_index("ex"))
    table = jnp.array([place[mask] for mask in range(len(place))], dtype=jnp.int32)
    return jnp.concatenate(parts, axis=0)[table[device]]


def join_kernel(hidden, inputs, out, sems):
    width_h = hidden.shape[1]
    copies = [
        pltpu.make_async_copy(hidden, out.at[:, :width_h], sems.at[0]),
        pltpu.make_async_copy(inputs, out.at[:, width_h:], sems.at[1]),
    ]
    for copy in copies:
        copy.start()
    for copy in copies:
        copy.wait()


def self_kernel(train_h, train_i, eig_h, eig_i, ids, out):
    def pairs(train, eig):
        values = train[...]
        scaled = (values.astype(jnp.float32) * (1.0 / (eig[...] + DAMP))).astype(jnp.bfloat16)
        return lax.dot_general(scaled, values, BY_LANES, preferred_element_type=jnp.float32)

    own_pairs = pairs(train_h, eig_h) * pairs(train_i, eig_i)
    row = lax.broadcasted_iota(jnp.int32, (out.shape[0], ids.shape[1]), 0)
    hot = (ids[...] == row - E_DEV).astype(jnp.float32)
    sums = jnp.dot(
        hot, own_pairs, precision=lax.Precision.HIGHEST, preferred_element_type=jnp.float32
    )
    out[...] = jnp.broadcast_to(jnp.sum(sums * hot, axis=1, keepdims=True), out.shape)


def rotate_kernel(masks, *refs):
    parts = refs[:-7]
    basis_h, basis_i, eig_h, eig_i, _, out, tokens = refs[-7:]
    width_h = basis_h.shape[0]
    hid_block = basis_h.shape[1]
    inp_block = basis_i.shape[1]
    me = lax.axis_index("ex")
    for part, of_part in zip(parts, masks):
        for i, mask in enumerate(of_part):
            tokens[me ^ mask] = part[i]

    def rotate(lanes, basis, eig, block, to):
        in_order = jnp.concatenate([tokens[k, :, lanes] for k in range(tokens.shape[0])], axis=0)
        product = jnp.dot(in_order, basis[...], preferred_element_type=jnp.float32)
        at = pl.ds(pl.multiple_of(me * block, LANES), block)
        out[0, :, to] = (product * (1.0 / (eig[:, at] + DAMP))).astype(jnp.bfloat16)

    rotate(slice(0, width_h), basis_h, eig_h, hid_block, slice(0, hid_block))
    rotate(slice(width_h, None), basis_i, eig_i, inp_block, slice(hid_block, None))


def add_grams(grams, masks, parts, train_h, train_i):
    me = lax.axis_index("ex")
    trains = (train_h, train_i)
    ends = [train.shape[1] // lax.axis_size("ex") for train in trains]
    lanes = (slice(0, ends[0]), slice(ends[0], None))
    for part, of_part in zip(parts, masks):
        for i, mask in enumerate(of_part):
            block = me ^ mask
            grams = [
                gram
                + lax.dot_general(
                    part[i, :, at],
                    train[:, pl.ds(pl.multiple_of(block * size, LANES), size)],
                    BY_LANES,
                    preferred_element_type=jnp.float32,
                )
                for gram, train, size, at in zip(grams, trains, ends, lanes)
            ]
    return grams


def early_kernel(masks, *refs):
    parts = refs[:-5]
    train_h, train_i, query_ids, grams, query_hot = refs[-5:]
    grams[0], grams[1] = add_grams((0.0, 0.0), masks, parts, train_h, train_i)
    tokens = query_ids.shape[1]
    row = lax.broadcasted_iota(jnp.int32, (tokens, tokens), 0)
    column = lax.broadcasted_iota(jnp.int32, (tokens, tokens), 1)
    own_id = jnp.where(row == column, jnp.broadcast_to(query_ids[...], (tokens, tokens)), 0)
    own_id = jnp.sum(own_id.astype(jnp.float32), axis=1, keepdims=True)
    query = lax.broadcasted_iota(jnp.int32, query_hot.shape, 1).astype(jnp.float32)
    query_hot[...] = (own_id == query).astype(jnp.float32)


def more_kernel(masks, *refs):
    parts = refs[:-4]
    train_h, train_i, grams, out = refs[-4:]
    out[0], out[1] = add_grams((grams[0], grams[1]), masks, parts, train_h, train_i)


def late_kernel(masks, *refs):
    parts = refs[:-7]
    train_h, train_i, grams, query_hot, ids, own_self, out = refs[-7:]
    gram_h, gram_i = add_grams((grams[0], grams[1]), masks, parts, train_h, train_i)
    cross = gram_h * gram_i
    row = lax.broadcasted_iota(jnp.int32, out.shape, 0)
    scores = own_self[...]
    for e in range(E_DEV):
        of_token = jnp.sum(jnp.where(ids[...] == e, cross, 0.0), axis=1, keepdims=True)
        of_query = jnp.sum(of_token * query_hot[...], axis=0, keepdims=True)
        scores = jnp.where(row == e, of_query, scores)
    out[...] = scores


def finish_kernel(mine, other, out):
    total = mine[...] + other[...]
    half = QUERIES // 2
    relative = total[:E_DEV] / jnp.sqrt(total[E_DEV : 2 * E_DEV] + 1e-06)
    out[...] = jnp.where(
        lax.axis_index("layer") == 0, relative[:, :half], relative[:, half:QUERIES]
    )


def call(kernel, name, out_shape, flops=0, moved=0, **more):
    return pl.pallas_call(
        kernel,
        out_shape=out_shape,
        name=name,
        compiler_params=pltpu.CompilerParams(vmem_limit_bytes=8 * MIB),
        cost_estimate=pl.CostEstimate(flops=flops, bytes_accessed=moved, transcendentals=0),
        **more,
    )


def layer_swap(x):
    return lax.ppermute(x, "layer", [(0, 1), (1, 0)])


def body(
    query_out_grads,
    query_inputs,
    train_out_grads,
    train_inputs,
    basis_hidden,
    basis_inputs,
    eig_hidden,
    eig_inputs,
    query_ids,
    example_ids,
):
    shards = lax.axis_size("ex")
    hid_block = basis_hidden.shape[2]
    inp_block = basis_inputs.shape[2]
    rest = (
        train_out_grads[0],
        train_inputs[0],
        basis_hidden[0],
        basis_inputs[0],
        eig_hidden,
        eig_inputs,
        query_ids[None, :],
        example_ids,
    )
    if hid_block % LANES or inp_block % LANES:
        own = jnp.concatenate([query_out_grads[0], query_inputs[0]], axis=1)
        return plain(own, *rest)
    train_h, train_i, basis_h, basis_i, eig_h, eig_i, query_ids, example_ids = map(vmem, rest)
    own_tokens = query_inputs.shape[1]
    width = query_out_grads.shape[2] + query_inputs.shape[2]
    tokens = own_tokens * shards
    own = call(
        join_kernel,
        "join",
        pltpu.VMEM((own_tokens, width), jnp.bfloat16),
        flops=20_000_000_000,
        in_specs=[pl.BlockSpec(memory_space=pl.ANY)] * 2,
        out_specs=pl.BlockSpec(memory_space=pltpu.VMEM),
        scratch_shapes=[pltpu.SemaphoreType.DMA((2,))],
    )(hbm(query_out_grads[0]), hbm(query_inputs[0]))
    everyone, masks = gather(own, shards, by_kernel=True)
    small = jax.ShapeDtypeStruct((8, LANES), jnp.float32)
    own_self = call(
        self_kernel, "self_influence", small, flops=2 * 160 * 160 * 11264, moved=3_700_000
    )(train_h, train_i, eig_h, eig_i, example_ids)
    rotated = call(
        functools.partial(rotate_kernel, masks),
        "rotate",
        jax.ShapeDtypeStruct((1, tokens, hid_block + inp_block), jnp.bfloat16),
        flops=2 * 16 * 8_500_000,
        moved=17_000_000,
        scratch_shapes=[pltpu.VMEM((shards, own_tokens, width), jnp.bfloat16)],
    )(*everyone, basis_h, basis_i, eig_h, eig_i, own_self)
    parts, masks = gather(rotated[0], shards, ROTATED_PLAN)
    gram_shape = jax.ShapeDtypeStruct((2, tokens, train_h.shape[0]), jnp.float32)
    first, last = 3, 4
    grams, query_hot = call(
        functools.partial(early_kernel, masks[:first]),
        "early_grams",
        (gram_shape, jax.ShapeDtypeStruct((tokens, LANES), jnp.float32)),
        flops=500_000_000,
    )(*parts[:first], train_h, train_i, query_ids)
    grams = call(functools.partial(more_kernel, masks[first:last]), "more_grams", gram_shape, flops=300_000_000)(
        *parts[first:last], train_h, train_i, grams
    )
    mine = call(functools.partial(late_kernel, masks[last:]), "scores", small)(
        *parts[last:], train_h, train_i, grams, query_hot, example_ids, own_self
    )
    return call(
        finish_kernel,
        "finish",
        jax.ShapeDtypeStruct((E_DEV, QUERIES // 2), jnp.float32),
    )(mine, layer_swap(mine)).T


def plain(own, train_h, train_i, basis_h, basis_i, eig_h, eig_i, query_ids, example_ids):
    shards = lax.axis_size("ex")
    my_index = lax.axis_index("ex")
    width_h, hid_block = basis_h.shape
    inp_block = basis_i.shape[1]
    everyone = in_order(*gather(own, shards)).reshape(-1, own.shape[1])
    gain_h = 1.0 / (eig_h + DAMP)
    gain_i = 1.0 / (eig_i + DAMP)

    def rotate(tokens, basis, gain, block):
        product = jnp.dot(tokens, basis, preferred_element_type=jnp.float32)
        own_gain = lax.dynamic_slice_in_dim(gain, my_index * block, block, 1)
        return (product * own_gain).astype(jnp.bfloat16)

    rot_h = rotate(everyone[:, :width_h], basis_h, gain_h, hid_block)
    rot_i = rotate(everyone[:, width_h:], basis_i, gain_i, inp_block)
    pieces = in_order(*gather(jnp.concatenate([rot_h, rot_i], axis=1), shards))

    def gram(piece, train):
        split = train.reshape(train.shape[0], shards, -1)
        return jnp.einsum("nqf,tnf->qt", piece, split, preferred_element_type=jnp.float32)

    cross = gram(pieces[:, :, :hid_block], train_h) * gram(pieces[:, :, hid_block:], train_i)
    query_hot = query_ids == jnp.arange(QUERIES, dtype=jnp.int32)[:, None]
    example_hot = (example_ids == jnp.arange(E_DEV, dtype=jnp.int32)[:, None]).astype(jnp.float32)
    summed = jnp.dot(query_hot.astype(jnp.float32), cross, precision=lax.Precision.HIGHEST)
    scores = jnp.dot(summed, example_hot.T, precision=lax.Precision.HIGHEST)

    def pairs(train, gain):
        scaled = (train * gain).astype(jnp.bfloat16)
        return jnp.dot(scaled, train.T, preferred_element_type=jnp.float32)

    own_pairs = pairs(train_h, gain_h) * pairs(train_i, gain_i)
    sums = jnp.dot(example_hot, own_pairs, precision=lax.Precision.HIGHEST)
    own_self = jnp.sum(sums * example_hot, axis=1)
    mine = jnp.concatenate([scores, jnp.broadcast_to(own_self, scores.shape)], axis=1)
    total = mine + layer_swap(mine)
    half = QUERIES // 2
    total = lax.dynamic_slice_in_dim(total, lax.axis_index("layer") * half, half, 0)
    return total[:, :E_DEV] / jnp.sqrt(total[:, E_DEV:] + 1e-06)


def solution(mesh):
    in_specs = (
        P("layer", ("groups", "ex"), None),
        P("layer", ("groups", "ex"), None),
        P("layer", ("groups", "ex"), None),
        P("layer", ("groups", "ex"), None),
        P("layer", None, "ex"),
        P("layer", None, "ex"),
        P("layer", None),
        P("layer", None),
        P("groups"),
        P(("groups", "ex"), None),
    )
    out_specs = P(("groups", "layer"), "ex")
    return jax.shard_map(body, mesh=mesh, in_specs=in_specs, out_specs=out_specs, check_vma=False)
```

```python
import functools

import jax
import jax.numpy as jnp
from jax import lax
from jax.experimental import pallas as pl
from jax.experimental.pallas import tpu as pltpu
from jax.sharding import PartitionSpec as P

E_DEV = 2
QUERIES = 8
DAMP = 0.1
LANES = 128
MIB = 2**20
X, Z, FAR = 1, 2, 4
QUERY_PLAN = [(FAR, (0,)), (X, (0,)), (Z, (0, X)), (Z ^ FAR, (0, X)), (X, (FAR,))]
ROTATED_PLAN = [(FAR, (0,)), (X, (0,)), (Z ^ FAR, (0, X)), (X, (FAR,)), (Z, (0, X))]
BY_LANES = (((1,), (1,)), ((), ()))


def vmem(x):
    return pltpu.with_memory_space_constraint(x, pltpu.VMEM)


def hbm(x):
    return pltpu.with_memory_space_constraint(x, pltpu.HBM)


def steps(shards, plan):
    if shards == 8:
        return plan
    plan, known, stride = [], [0], shards
    while stride > 1:
        radix = min(4, stride)
        stride //= radix
        plan += [(m * stride, tuple(known)) for m in range(1, radix)]
        known = [k ^ (m * stride) for m in range(radix) for k in known]
    return plan


def gather(x, shards, plan=QUERY_PLAN, by_kernel=False):
    x = x[None]
    parts, masks = [x], [[0]]
    blocks, joined = {0: x}, {(0,): x}
    for mask, sent in steps(shards, plan):
        if sent not in joined:
            if by_kernel and len(sent) == 2:
                joined[sent] = call(
                    pair_kernel, "pair", jax.ShapeDtypeStruct((2, *x.shape[1:]), x.dtype)
                )(*[blocks[s] for s in sent])
            else:
                joined[sent] = jnp.concatenate([blocks[s] for s in sent], axis=0)
        part = lax.ppermute(joined[sent], "ex", [(i, i ^ mask) for i in range(shards)])
        parts.append(part)
        masks.append([mask ^ s for s in sent])
        for i, s in enumerate(sent):
            blocks[mask ^ s] = part[i : i + 1]
    return parts, masks


def pair_kernel(first, second, out):
    out[:1] = first[...]
    out[1:] = second[...]


def in_order(parts, masks):
    place = {mask: at for at, mask in enumerate(sum(masks, []))}
    device = jnp.bitwise_xor(jnp.arange(len(place), dtype=jnp.int32), lax.axis_index("ex"))
    table = jnp.array([place[mask] for mask in range(len(place))], dtype=jnp.int32)
    return jnp.concatenate(parts, axis=0)[table[device]]


def join_kernel(hidden, inputs, out, sems):
    width_h = hidden.shape[1]
    copies = [
        pltpu.make_async_copy(hidden, out.at[:, :width_h], sems.at[0]),
        pltpu.make_async_copy(inputs, out.at[:, width_h:], sems.at[1]),
    ]
    for copy in copies:
        copy.start()
    for copy in copies:
        copy.wait()


def self_kernel(train_h, train_i, eig_h, eig_i, ids, out):
    def pairs(train, eig):
        values = train[...]
        scaled = (values.astype(jnp.float32) * (1.0 / (eig[...] + DAMP))).astype(jnp.bfloat16)
        return lax.dot_general(scaled, values, BY_LANES, preferred_element_type=jnp.float32)

    own_pairs = pairs(train_h, eig_h) * pairs(train_i, eig_i)
    row = lax.broadcasted_iota(jnp.int32, (out.shape[0], ids.shape[1]), 0)
    hot = (ids[...] == row - E_DEV).astype(jnp.float32)
    sums = jnp.dot(
        hot, own_pairs, precision=lax.Precision.HIGHEST, preferred_element_type=jnp.float32
    )
    out[...] = jnp.broadcast_to(jnp.sum(sums * hot, axis=1, keepdims=True), out.shape)


def rotate_kernel(masks, *refs):
    parts = refs[:-7]
    basis_h, basis_i, eig_h, eig_i, _, out, tokens = refs[-7:]
    width_h = basis_h.shape[0]
    hid_block = basis_h.shape[1]
    inp_block = basis_i.shape[1]
    me = lax.axis_index("ex")
    for part, of_part in zip(parts, masks):
        for i, mask in enumerate(of_part):
            tokens[me ^ mask] = part[i]

    def rotate(lanes, basis, eig, block, to):
        in_order = jnp.concatenate([tokens[k, :, lanes] for k in range(tokens.shape[0])], axis=0)
        product = jnp.dot(in_order, basis[...], preferred_element_type=jnp.float32)
        at = pl.ds(pl.multiple_of(me * block, LANES), block)
        out[0, :, to] = (product * (1.0 / (eig[:, at] + DAMP))).astype(jnp.bfloat16)

    rotate(slice(0, width_h), basis_h, eig_h, hid_block, slice(0, hid_block))
    rotate(slice(width_h, None), basis_i, eig_i, inp_block, slice(hid_block, None))


def add_grams(grams, masks, parts, train_h, train_i):
    me = lax.axis_index("ex")
    trains = (train_h, train_i)
    ends = [train.shape[1] // lax.axis_size("ex") for train in trains]
    lanes = (slice(0, ends[0]), slice(ends[0], None))
    for part, of_part in zip(parts, masks):
        for i, mask in enumerate(of_part):
            block = me ^ mask
            grams = [
                gram
                + lax.dot_general(
                    part[i, :, at],
                    train[:, pl.ds(pl.multiple_of(block * size, LANES), size)],
                    BY_LANES,
                    preferred_element_type=jnp.float32,
                )
                for gram, train, size, at in zip(grams, trains, ends, lanes)
            ]
    return grams


def early_kernel(masks, *refs):
    parts = refs[:-5]
    train_h, train_i, query_ids, grams, query_hot = refs[-5:]
    grams[0], grams[1] = add_grams((0.0, 0.0), masks, parts, train_h, train_i)
    tokens = query_ids.shape[1]
    row = lax.broadcasted_iota(jnp.int32, (tokens, tokens), 0)
    column = lax.broadcasted_iota(jnp.int32, (tokens, tokens), 1)
    own_id = jnp.where(row == column, jnp.broadcast_to(query_ids[...], (tokens, tokens)), 0)
    own_id = jnp.sum(own_id.astype(jnp.float32), axis=1, keepdims=True)
    query = lax.broadcasted_iota(jnp.int32, query_hot.shape, 1).astype(jnp.float32)
    query_hot[...] = (own_id == query).astype(jnp.float32)


def more_kernel(masks, *refs):
    parts = refs[:-4]
    train_h, train_i, grams, out = refs[-4:]
    out[0], out[1] = add_grams((grams[0], grams[1]), masks, parts, train_h, train_i)


def late_kernel(masks, *refs):
    parts = refs[:-7]
    train_h, train_i, grams, query_hot, ids, own_self, out = refs[-7:]
    gram_h, gram_i = add_grams((grams[0], grams[1]), masks, parts, train_h, train_i)
    cross = gram_h * gram_i
    row = lax.broadcasted_iota(jnp.int32, out.shape, 0)
    scores = own_self[...]
    for e in range(E_DEV):
        of_token = jnp.sum(jnp.where(ids[...] == e, cross, 0.0), axis=1, keepdims=True)
        of_query = jnp.sum(of_token * query_hot[...], axis=0, keepdims=True)
        scores = jnp.where(row == e, of_query, scores)
    out[...] = scores


def finish_kernel(mine, other, out):
    total = mine[...] + other[...]
    half = QUERIES // 2
    relative = total[:E_DEV] / jnp.sqrt(total[E_DEV : 2 * E_DEV] + 1e-06)
    out[...] = jnp.where(
        lax.axis_index("layer") == 0, relative[:, :half], relative[:, half:QUERIES]
    )


def call(kernel, name, out_shape, flops=0, moved=0, **more):
    return pl.pallas_call(
        kernel,
        out_shape=out_shape,
        name=name,
        compiler_params=pltpu.CompilerParams(vmem_limit_bytes=8 * MIB),
        cost_estimate=pl.CostEstimate(flops=flops, bytes_accessed=moved, transcendentals=0),
        **more,
    )


def layer_swap(x):
    return lax.ppermute(x, "layer", [(0, 1), (1, 0)])


def body(
    query_out_grads,
    query_inputs,
    train_out_grads,
    train_inputs,
    basis_hidden,
    basis_inputs,
    eig_hidden,
    eig_inputs,
    query_ids,
    example_ids,
):
    shards = lax.axis_size("ex")
    hid_block = basis_hidden.shape[2]
    inp_block = basis_inputs.shape[2]
    rest = (
        train_out_grads[0],
        train_inputs[0],
        basis_hidden[0],
        basis_inputs[0],
        eig_hidden,
        eig_inputs,
        query_ids[None, :],
        example_ids,
    )
    if hid_block % LANES or inp_block % LANES:
        own = jnp.concatenate([query_out_grads[0], query_inputs[0]], axis=1)
        return plain(own, *rest)
    train_h, train_i, basis_h, basis_i, eig_h, eig_i, query_ids, example_ids = map(vmem, rest)
    own_tokens = query_inputs.shape[1]
    width = query_out_grads.shape[2] + query_inputs.shape[2]
    tokens = own_tokens * shards
    own = call(
        join_kernel,
        "join",
        pltpu.VMEM((own_tokens, width), jnp.bfloat16),
        flops=20_000_000_000,
        in_specs=[pl.BlockSpec(memory_space=pl.ANY)] * 2,
        out_specs=pl.BlockSpec(memory_space=pltpu.VMEM),
        scratch_shapes=[pltpu.SemaphoreType.DMA((2,))],
    )(hbm(query_out_grads[0]), hbm(query_inputs[0]))
    everyone, masks = gather(own, shards, by_kernel=True)
    small = jax.ShapeDtypeStruct((8, LANES), jnp.float32)
    own_self = call(
        self_kernel, "self_influence", small, flops=2 * 160 * 160 * 11264, moved=3_700_000
    )(train_h, train_i, eig_h, eig_i, example_ids)
    rotated = call(
        functools.partial(rotate_kernel, masks),
        "rotate",
        jax.ShapeDtypeStruct((1, tokens, hid_block + inp_block), jnp.bfloat16),
        flops=2 * 16 * 8_500_000,
        moved=17_000_000,
        scratch_shapes=[pltpu.VMEM((shards, own_tokens, width), jnp.bfloat16)],
    )(*everyone, basis_h, basis_i, eig_h, eig_i, own_self)
    parts, masks = gather(rotated[0], shards, ROTATED_PLAN)
    gram_shape = jax.ShapeDtypeStruct((2, tokens, train_h.shape[0]), jnp.float32)
    first, last = 3, 4
    grams, query_hot = call(
        functools.partial(early_kernel, masks[:first]),
        "early_grams",
        (gram_shape, jax.ShapeDtypeStruct((tokens, LANES), jnp.float32)),
        flops=500_000_000,
    )(*parts[:first], train_h, train_i, query_ids)
    grams = call(functools.partial(more_kernel, masks[first:last]), "more_grams", gram_shape, flops=300_000_000)(
        *parts[first:last], train_h, train_i, grams
    )
    mine = call(functools.partial(late_kernel, masks[last:]), "scores", small)(
        *parts[last:], train_h, train_i, grams, query_hot, example_ids, own_self
    )
    return call(
        finish_kernel,
        "finish",
        jax.ShapeDtypeStruct((E_DEV, QUERIES // 2), jnp.float32),
    )(mine, layer_swap(mine)).T


def plain(own, train_h, train_i, basis_h, basis_i, eig_h, eig_i, query_ids, example_ids):
    shards = lax.axis_size("ex")
    my_index = lax.axis_index("ex")
    width_h, hid_block = basis_h.shape
    inp_block = basis_i.shape[1]
    everyone = in_order(*gather(own, shards)).reshape(-1, own.shape[1])
    gain_h = 1.0 / (eig_h + DAMP)
    gain_i = 1.0 / (eig_i + DAMP)

    def rotate(tokens, basis, gain, block):
        product = jnp.dot(tokens, basis, preferred_element_type=jnp.float32)
        own_gain = lax.dynamic_slice_in_dim(gain, my_index * block, block, 1)
        return (product * own_gain).astype(jnp.bfloat16)

    rot_h = rotate(everyone[:, :width_h], basis_h, gain_h, hid_block)
    rot_i = rotate(everyone[:, width_h:], basis_i, gain_i, inp_block)
    pieces = in_order(*gather(jnp.concatenate([rot_h, rot_i], axis=1), shards))

    def gram(piece, train):
        split = train.reshape(train.shape[0], shards, -1)
        return jnp.einsum("nqf,tnf->qt", piece, split, preferred_element_type=jnp.float32)

    cross = gram(pieces[:, :, :hid_block], train_h) * gram(pieces[:, :, hid_block:], train_i)
    query_hot = query_ids == jnp.arange(QUERIES, dtype=jnp.int32)[:, None]
    example_hot = (example_ids == jnp.arange(E_DEV, dtype=jnp.int32)[:, None]).astype(jnp.float32)
    summed = jnp.dot(query_hot.astype(jnp.float32), cross, precision=lax.Precision.HIGHEST)
    scores = jnp.dot(summed, example_hot.T, precision=lax.Precision.HIGHEST)

    def pairs(train, gain):
        scaled = (train * gain).astype(jnp.bfloat16)
        return jnp.dot(scaled, train.T, preferred_element_type=jnp.float32)

    own_pairs = pairs(train_h, gain_h) * pairs(train_i, gain_i)
    sums = jnp.dot(example_hot, own_pairs, precision=lax.Precision.HIGHEST)
    own_self = jnp.sum(sums * example_hot, axis=1)
    mine = jnp.concatenate([scores, jnp.broadcast_to(own_self, scores.shape)], axis=1)
    total = mine + layer_swap(mine)
    half = QUERIES // 2
    total = lax.dynamic_slice_in_dim(total, lax.axis_index("layer") * half, half, 0)
    return total[:, :E_DEV] / jnp.sqrt(total[:, E_DEV:] + 1e-06)


def solution(mesh):
    in_specs = (
        P("layer", ("groups", "ex"), None),
        P("layer", ("groups", "ex"), None),
        P("layer", ("groups", "ex"), None),
        P("layer", ("groups", "ex"), None),
        P("layer", None, "ex"),
        P("layer", None, "ex"),
        P("layer", None),
        P("layer", None),
        P("groups"),
        P(("groups", "ex"), None),
    )
    out_specs = P(("groups", "layer"), "ex")
    return jax.shard_map(body, mesh=mesh, in_specs=in_specs, out_specs=out_specs, check_vma=False)
```

```python
import functools

import jax
import jax.numpy as jnp
from jax import lax
from jax.experimental import pallas as pl
from jax.experimental.pallas import tpu as pltpu
from jax.sharding import PartitionSpec as P

E_DEV = 2
QUERIES = 8
DAMP = 0.1
LANES = 128
MIB = 2**20
X, Z, FAR = 1, 2, 4
QUERY_PLAN = [(FAR, (0,)), (X, (0,)), (Z, (0, X)), (Z ^ FAR, (0, X)), (X, (FAR,))]
ROTATED_PLAN = [(FAR, (0,)), (X, (0,)), (Z ^ FAR, (0, X)), (X, (FAR,)), (Z, (0, X))]
BY_LANES = (((1,), (1,)), ((), ()))


def vmem(x):
    return pltpu.with_memory_space_constraint(x, pltpu.VMEM)


def hbm(x):
    return pltpu.with_memory_space_constraint(x, pltpu.HBM)


def steps(shards, plan):
    if shards == 8:
        return plan
    plan, known, stride = [], [0], shards
    while stride > 1:
        radix = min(4, stride)
        stride //= radix
        plan += [(m * stride, tuple(known)) for m in range(1, radix)]
        known = [k ^ (m * stride) for m in range(radix) for k in known]
    return plan


def gather(x, shards, plan=QUERY_PLAN, by_kernel=False):
    x = x[None]
    parts, masks = [x], [[0]]
    blocks, joined = {0: x}, {(0,): x}
    for mask, sent in steps(shards, plan):
        if sent not in joined:
            if by_kernel and len(sent) == 2:
                joined[sent] = call(
                    pair_kernel, "pair", jax.ShapeDtypeStruct((2, *x.shape[1:]), x.dtype)
                )(*[blocks[s] for s in sent])
            else:
                joined[sent] = jnp.concatenate([blocks[s] for s in sent], axis=0)
        part = lax.ppermute(joined[sent], "ex", [(i, i ^ mask) for i in range(shards)])
        parts.append(part)
        masks.append([mask ^ s for s in sent])
        for i, s in enumerate(sent):
            blocks[mask ^ s] = part[i : i + 1]
    return parts, masks


def pair_kernel(first, second, out):
    out[:1] = first[...]
    out[1:] = second[...]


def in_order(parts, masks):
    place = {mask: at for at, mask in enumerate(sum(masks, []))}
    device = jnp.bitwise_xor(jnp.arange(len(place), dtype=jnp.int32), lax.axis_index("ex"))
    table = jnp.array([place[mask] for mask in range(len(place))], dtype=jnp.int32)
    return jnp.concatenate(parts, axis=0)[table[device]]


def join_kernel(hidden, inputs, out, sems):
    width_h = hidden.shape[1]
    copies = [
        pltpu.make_async_copy(hidden, out.at[:, :width_h], sems.at[0]),
        pltpu.make_async_copy(inputs, out.at[:, width_h:], sems.at[1]),
    ]
    for copy in copies:
        copy.start()
    for copy in copies:
        copy.wait()


def self_kernel(train_h, train_i, eig_h, eig_i, ids, out):
    def pairs(train, eig):
        values = train[...]
        scaled = (values.astype(jnp.float32) * (1.0 / (eig[...] + DAMP))).astype(jnp.bfloat16)
        return lax.dot_general(scaled, values, BY_LANES, preferred_element_type=jnp.float32)

    own_pairs = pairs(train_h, eig_h) * pairs(train_i, eig_i)
    row = lax.broadcasted_iota(jnp.int32, (out.shape[0], ids.shape[1]), 0)
    hot = (ids[...] == row - E_DEV).astype(jnp.float32)
    sums = jnp.dot(
        hot, own_pairs, precision=lax.Precision.HIGHEST, preferred_element_type=jnp.float32
    )
    out[...] = jnp.broadcast_to(jnp.sum(sums * hot, axis=1, keepdims=True), out.shape)


def rotate_kernel(masks, *refs):
    parts = refs[:-7]
    basis_h, basis_i, eig_h, eig_i, _, out, tokens = refs[-7:]
    width_h = basis_h.shape[0]
    hid_block = basis_h.shape[1]
    inp_block = basis_i.shape[1]
    me = lax.axis_index("ex")
    for part, of_part in zip(parts, masks):
        for i, mask in enumerate(of_part):
            tokens[me ^ mask] = part[i]

    def rotate(lanes, basis, eig, block, to):
        in_order = jnp.concatenate([tokens[k, :, lanes] for k in range(tokens.shape[0])], axis=0)
        product = jnp.dot(in_order, basis[...], preferred_element_type=jnp.float32)
        at = pl.ds(pl.multiple_of(me * block, LANES), block)
        out[0, :, to] = (product * (1.0 / (eig[:, at] + DAMP))).astype(jnp.bfloat16)

    rotate(slice(0, width_h), basis_h, eig_h, hid_block, slice(0, hid_block))
    rotate(slice(width_h, None), basis_i, eig_i, inp_block, slice(hid_block, None))


def add_grams(grams, masks, parts, train_h, train_i):
    me = lax.axis_index("ex")
    trains = (train_h, train_i)
    ends = [train.shape[1] // lax.axis_size("ex") for train in trains]
    lanes = (slice(0, ends[0]), slice(ends[0], None))
    for part, of_part in zip(parts, masks):
        for i, mask in enumerate(of_part):
            block = me ^ mask
            grams = [
                gram
                + lax.dot_general(
                    part[i, :, at],
                    train[:, pl.ds(pl.multiple_of(block * size, LANES), size)],
                    BY_LANES,
                    preferred_element_type=jnp.float32,
                )
                for gram, train, size, at in zip(grams, trains, ends, lanes)
            ]
    return grams


def early_kernel(masks, *refs):
    parts = refs[:-5]
    train_h, train_i, query_ids, grams, query_hot = refs[-5:]
    grams[0], grams[1] = add_grams((0.0, 0.0), masks, parts, train_h, train_i)
    tokens = query_ids.shape[1]
    row = lax.broadcasted_iota(jnp.int32, (tokens, tokens), 0)
    column = lax.broadcasted_iota(jnp.int32, (tokens, tokens), 1)
    own_id = jnp.where(row == column, jnp.broadcast_to(query_ids[...], (tokens, tokens)), 0)
    own_id = jnp.sum(own_id.astype(jnp.float32), axis=1, keepdims=True)
    query = lax.broadcasted_iota(jnp.int32, query_hot.shape, 1).astype(jnp.float32)
    query_hot[...] = (own_id == query).astype(jnp.float32)


def more_kernel(masks, *refs):
    parts = refs[:-4]
    train_h, train_i, grams, out = refs[-4:]
    out[0], out[1] = add_grams((grams[0], grams[1]), masks, parts, train_h, train_i)


def late_kernel(masks, *refs):
    parts = refs[:-7]
    train_h, train_i, grams, query_hot, ids, own_self, out = refs[-7:]
    gram_h, gram_i = add_grams((grams[0], grams[1]), masks, parts, train_h, train_i)
    cross = gram_h * gram_i
    row = lax.broadcasted_iota(jnp.int32, out.shape, 0)
    scores = own_self[...]
    for e in range(E_DEV):
        of_token = jnp.sum(jnp.where(ids[...] == e, cross, 0.0), axis=1, keepdims=True)
        of_query = jnp.sum(of_token * query_hot[...], axis=0, keepdims=True)
        scores = jnp.where(row == e, of_query, scores)
    out[...] = scores


def finish_kernel(mine, other, out):
    total = mine[...] + other[...]
    half = QUERIES // 2
    relative = total[:E_DEV] / jnp.sqrt(total[E_DEV : 2 * E_DEV] + 1e-06)
    out[...] = jnp.where(
        lax.axis_index("layer") == 0, relative[:, :half], relative[:, half:QUERIES]
    )


def call(kernel, name, out_shape, flops=0, moved=0, **more):
    return pl.pallas_call(
        kernel,
        out_shape=out_shape,
        name=name,
        compiler_params=pltpu.CompilerParams(vmem_limit_bytes=8 * MIB),
        cost_estimate=pl.CostEstimate(flops=flops, bytes_accessed=moved, transcendentals=0),
        **more,
    )


def layer_swap(x):
    return lax.ppermute(x, "layer", [(0, 1), (1, 0)])


def body(
    query_out_grads,
    query_inputs,
    train_out_grads,
    train_inputs,
    basis_hidden,
    basis_inputs,
    eig_hidden,
    eig_inputs,
    query_ids,
    example_ids,
):
    shards = lax.axis_size("ex")
    hid_block = basis_hidden.shape[2]
    inp_block = basis_inputs.shape[2]
    rest = (
        train_out_grads[0],
        train_inputs[0],
        basis_hidden[0],
        basis_inputs[0],
        eig_hidden,
        eig_inputs,
        query_ids[None, :],
        example_ids,
    )
    if hid_block % LANES or inp_block % LANES:
        own = jnp.concatenate([query_out_grads[0], query_inputs[0]], axis=1)
        return plain(own, *rest)
    train_h, train_i, basis_h, basis_i, eig_h, eig_i, query_ids, example_ids = map(vmem, rest)
    own_tokens = query_inputs.shape[1]
    width = query_out_grads.shape[2] + query_inputs.shape[2]
    tokens = own_tokens * shards
    own = call(
        join_kernel,
        "join",
        pltpu.VMEM((own_tokens, width), jnp.bfloat16),
        flops=20_000_000_000,
        in_specs=[pl.BlockSpec(memory_space=pl.ANY)] * 2,
        out_specs=pl.BlockSpec(memory_space=pltpu.VMEM),
        scratch_shapes=[pltpu.SemaphoreType.DMA((2,))],
    )(hbm(query_out_grads[0]), hbm(query_inputs[0]))
    everyone, masks = gather(own, shards, by_kernel=True)
    small = jax.ShapeDtypeStruct((8, LANES), jnp.float32)
    own_self = call(
        self_kernel, "self_influence", small, flops=2 * 160 * 160 * 11264, moved=3_700_000
    )(train_h, train_i, eig_h, eig_i, example_ids)
    rotated = call(
        functools.partial(rotate_kernel, masks),
        "rotate",
        jax.ShapeDtypeStruct((1, tokens, hid_block + inp_block), jnp.bfloat16),
        flops=2 * 16 * 8_500_000,
        moved=17_000_000,
        scratch_shapes=[pltpu.VMEM((shards, own_tokens, width), jnp.bfloat16)],
    )(*everyone, basis_h, basis_i, eig_h, eig_i, own_self)
    parts, masks = gather(rotated[0], shards, ROTATED_PLAN)
    gram_shape = jax.ShapeDtypeStruct((2, tokens, train_h.shape[0]), jnp.float32)
    first, last = 3, 5
    grams, query_hot = call(
        functools.partial(early_kernel, masks[:first]),
        "early_grams",
        (gram_shape, jax.ShapeDtypeStruct((tokens, LANES), jnp.float32)),
        flops=500_000_000,
    )(*parts[:first], train_h, train_i, query_ids)
    grams = call(functools.partial(more_kernel, masks[first:last]), "more_grams", gram_shape, flops=300_000_000)(
        *parts[first:last], train_h, train_i, grams
    )
    mine = call(functools.partial(late_kernel, masks[last:]), "scores", small)(
        *parts[last:], train_h, train_i, grams, query_hot, example_ids, own_self
    )
    return call(
        finish_kernel,
        "finish",
        jax.ShapeDtypeStruct((E_DEV, QUERIES // 2), jnp.float32),
    )(mine, layer_swap(mine)).T


def plain(own, train_h, train_i, basis_h, basis_i, eig_h, eig_i, query_ids, example_ids):
    shards = lax.axis_size("ex")
    my_index = lax.axis_index("ex")
    width_h, hid_block = basis_h.shape
    inp_block = basis_i.shape[1]
    everyone = in_order(*gather(own, shards)).reshape(-1, own.shape[1])
    gain_h = 1.0 / (eig_h + DAMP)
    gain_i = 1.0 / (eig_i + DAMP)

    def rotate(tokens, basis, gain, block):
        product = jnp.dot(tokens, basis, preferred_element_type=jnp.float32)
        own_gain = lax.dynamic_slice_in_dim(gain, my_index * block, block, 1)
        return (product * own_gain).astype(jnp.bfloat16)

    rot_h = rotate(everyone[:, :width_h], basis_h, gain_h, hid_block)
    rot_i = rotate(everyone[:, width_h:], basis_i, gain_i, inp_block)
    pieces = in_order(*gather(jnp.concatenate([rot_h, rot_i], axis=1), shards))

    def gram(piece, train):
        split = train.reshape(train.shape[0], shards, -1)
        return jnp.einsum("nqf,tnf->qt", piece, split, preferred_element_type=jnp.float32)

    cross = gram(pieces[:, :, :hid_block], train_h) * gram(pieces[:, :, hid_block:], train_i)
    query_hot = query_ids == jnp.arange(QUERIES, dtype=jnp.int32)[:, None]
    example_hot = (example_ids == jnp.arange(E_DEV, dtype=jnp.int32)[:, None]).astype(jnp.float32)
    summed = jnp.dot(query_hot.astype(jnp.float32), cross, precision=lax.Precision.HIGHEST)
    scores = jnp.dot(summed, example_hot.T, precision=lax.Precision.HIGHEST)

    def pairs(train, gain):
        scaled = (train * gain).astype(jnp.bfloat16)
        return jnp.dot(scaled, train.T, preferred_element_type=jnp.float32)

    own_pairs = pairs(train_h, gain_h) * pairs(train_i, gain_i)
    sums = jnp.dot(example_hot, own_pairs, precision=lax.Precision.HIGHEST)
    own_self = jnp.sum(sums * example_hot, axis=1)
    mine = jnp.concatenate([scores, jnp.broadcast_to(own_self, scores.shape)], axis=1)
    total = mine + layer_swap(mine)
    half = QUERIES // 2
    total = lax.dynamic_slice_in_dim(total, lax.axis_index("layer") * half, half, 0)
    return total[:, :E_DEV] / jnp.sqrt(total[:, E_DEV:] + 1e-06)


def solution(mesh):
    in_specs = (
        P("layer", ("groups", "ex"), None),
        P("layer", ("groups", "ex"), None),
        P("layer", ("groups", "ex"), None),
        P("layer", ("groups", "ex"), None),
        P("layer", None, "ex"),
        P("layer", None, "ex"),
        P("layer", None),
        P("layer", None),
        P("groups"),
        P(("groups", "ex"), None),
    )
    out_specs = P(("groups", "layer"), "ex")
    return jax.shard_map(body, mesh=mesh, in_specs=in_specs, out_specs=out_specs, check_vma=False)
```

```python
import functools

import jax
import jax.numpy as jnp
from jax import lax
from jax.experimental import pallas as pl
from jax.experimental.pallas import tpu as pltpu
from jax.sharding import PartitionSpec as P

E_DEV = 2
QUERIES = 8
DAMP = 0.1
LANES = 128
MIB = 2**20
X, Z, FAR = 1, 2, 4
QUERY_PLAN = [(FAR, (0,)), (X, (0,)), (Z, (0, X)), (Z ^ FAR, (0, X)), (X, (FAR,))]
ROTATED_PLAN = [(FAR, (0,)), (X, (0,)), (Z ^ FAR, (0, X)), (Z, (0, X)), (X, (FAR,))]
BY_LANES = (((1,), (1,)), ((), ()))


def vmem(x):
    return pltpu.with_memory_space_constraint(x, pltpu.VMEM)


def hbm(x):
    return pltpu.with_memory_space_constraint(x, pltpu.HBM)


def steps(shards, plan):
    if shards == 8:
        return plan
    plan, known, stride = [], [0], shards
    while stride > 1:
        radix = min(4, stride)
        stride //= radix
        plan += [(m * stride, tuple(known)) for m in range(1, radix)]
        known = [k ^ (m * stride) for m in range(radix) for k in known]
    return plan


def gather(x, shards, plan=QUERY_PLAN, by_kernel=False):
    x = x[None]
    parts, masks = [x], [[0]]
    blocks, joined = {0: x}, {(0,): x}
    for mask, sent in steps(shards, plan):
        if sent not in joined:
            if by_kernel and len(sent) == 2:
                joined[sent] = call(
                    pair_kernel, "pair", jax.ShapeDtypeStruct((2, *x.shape[1:]), x.dtype)
                )(*[blocks[s] for s in sent])
            else:
                joined[sent] = jnp.concatenate([blocks[s] for s in sent], axis=0)
        part = lax.ppermute(joined[sent], "ex", [(i, i ^ mask) for i in range(shards)])
        parts.append(part)
        masks.append([mask ^ s for s in sent])
        for i, s in enumerate(sent):
            blocks[mask ^ s] = part[i : i + 1]
    return parts, masks


def pair_kernel(first, second, out):
    out[:1] = first[...]
    out[1:] = second[...]


def in_order(parts, masks):
    place = {mask: at for at, mask in enumerate(sum(masks, []))}
    device = jnp.bitwise_xor(jnp.arange(len(place), dtype=jnp.int32), lax.axis_index("ex"))
    table = jnp.array([place[mask] for mask in range(len(place))], dtype=jnp.int32)
    return jnp.concatenate(parts, axis=0)[table[device]]


def hand_on_kernel(block, out):
    out[...] = block[...]


def self_kernel(train_h, train_i, eig_h, eig_i, ids, out):
    def pairs(train, eig):
        values = train[...]
        scaled = (values.astype(jnp.float32) * (1.0 / (eig[...] + DAMP))).astype(jnp.bfloat16)
        return lax.dot_general(scaled, values, BY_LANES, preferred_element_type=jnp.float32)

    own_pairs = pairs(train_h, eig_h) * pairs(train_i, eig_i)
    row = lax.broadcasted_iota(jnp.int32, (out.shape[0], ids.shape[1]), 0)
    hot = (ids[...] == row - E_DEV).astype(jnp.float32)
    sums = jnp.dot(
        hot, own_pairs, precision=lax.Precision.HIGHEST, preferred_element_type=jnp.float32
    )
    out[...] = jnp.broadcast_to(jnp.sum(sums * hot, axis=1, keepdims=True), out.shape)


def rotate_kernel(masks, *refs):
    parts = refs[:-7]
    basis_h, basis_i, eig_h, eig_i, _, out, tokens = refs[-7:]
    width_h = basis_h.shape[0]
    hid_block = basis_h.shape[1]
    inp_block = basis_i.shape[1]
    me = lax.axis_index("ex")
    for part, of_part in zip(parts, masks):
        for i, mask in enumerate(of_part):
            tokens[me ^ mask] = part[i]

    def rotate(lanes, basis, eig, block, to):
        in_order = jnp.concatenate([tokens[k, :, lanes] for k in range(tokens.shape[0])], axis=0)
        product = jnp.dot(in_order, basis[...], preferred_element_type=jnp.float32)
        at = pl.ds(pl.multiple_of(me * block, LANES), block)
        out[0, :, to] = (product * (1.0 / (eig[:, at] + DAMP))).astype(jnp.bfloat16)

    rotate(slice(0, width_h), basis_h, eig_h, hid_block, slice(0, hid_block))
    rotate(slice(width_h, None), basis_i, eig_i, inp_block, slice(hid_block, None))


def add_grams(grams, masks, parts, train_h, train_i):
    me = lax.axis_index("ex")
    trains = (train_h, train_i)
    ends = [train.shape[1] // lax.axis_size("ex") for train in trains]
    lanes = (slice(0, ends[0]), slice(ends[0], None))
    for part, of_part in zip(parts, masks):
        for i, mask in enumerate(of_part):
            block = me ^ mask
            grams = [
                gram
                + lax.dot_general(
                    part[i, :, at],
                    train[:, pl.ds(pl.multiple_of(block * size, LANES), size)],
                    BY_LANES,
                    preferred_element_type=jnp.float32,
                )
                for gram, train, size, at in zip(grams, trains, ends, lanes)
            ]
    return grams


def early_kernel(masks, *refs):
    parts = refs[:-5]
    train_h, train_i, query_ids, grams, query_hot = refs[-5:]
    grams[0], grams[1] = add_grams((0.0, 0.0), masks, parts, train_h, train_i)
    tokens = query_ids.shape[1]
    row = lax.broadcasted_iota(jnp.int32, (tokens, tokens), 0)
    column = lax.broadcasted_iota(jnp.int32, (tokens, tokens), 1)
    own_id = jnp.where(row == column, jnp.broadcast_to(query_ids[...], (tokens, tokens)), 0)
    own_id = jnp.sum(own_id.astype(jnp.float32), axis=1, keepdims=True)
    query = lax.broadcasted_iota(jnp.int32, query_hot.shape, 1).astype(jnp.float32)
    query_hot[...] = (own_id == query).astype(jnp.float32)


def more_kernel(masks, *refs):
    parts = refs[:-4]
    train_h, train_i, grams, out = refs[-4:]
    out[0], out[1] = add_grams((grams[0], grams[1]), masks, parts, train_h, train_i)


def late_kernel(masks, *refs):
    parts = refs[:-7]
    train_h, train_i, grams, query_hot, ids, own_self, out = refs[-7:]
    gram_h, gram_i = add_grams((grams[0], grams[1]), masks, parts, train_h, train_i)
    cross = gram_h * gram_i
    row = lax.broadcasted_iota(jnp.int32, out.shape, 0)
    scores = own_self[...]
    for e in range(E_DEV):
        of_token = jnp.sum(jnp.where(ids[...] == e, cross, 0.0), axis=1, keepdims=True)
        of_query = jnp.sum(of_token * query_hot[...], axis=0, keepdims=True)
        scores = jnp.where(row == e, of_query, scores)
    out[...] = scores


def finish_kernel(mine, other, out):
    total = mine[...] + other[...]
    half = QUERIES // 2
    relative = total[:E_DEV] / jnp.sqrt(total[E_DEV : 2 * E_DEV] + 1e-06)
    out[...] = jnp.where(
        lax.axis_index("layer") == 0, relative[:, :half], relative[:, half:QUERIES]
    )


def call(kernel, name, out_shape, flops=0, moved=0, **more):
    return pl.pallas_call(
        kernel,
        out_shape=out_shape,
        name=name,
        compiler_params=pltpu.CompilerParams(vmem_limit_bytes=8 * MIB),
        cost_estimate=pl.CostEstimate(flops=flops, bytes_accessed=moved, transcendentals=0),
        **more,
    )


def layer_swap(x):
    return lax.ppermute(x, "layer", [(0, 1), (1, 0)])


def body(
    query_out_grads,
    query_inputs,
    train_out_grads,
    train_inputs,
    basis_hidden,
    basis_inputs,
    eig_hidden,
    eig_inputs,
    query_ids,
    example_ids,
):
    shards = lax.axis_size("ex")
    hid_block = basis_hidden.shape[2]
    inp_block = basis_inputs.shape[2]
    rest = (
        train_out_grads[0],
        train_inputs[0],
        basis_hidden[0],
        basis_inputs[0],
        eig_hidden,
        eig_inputs,
        query_ids[None, :],
        example_ids,
    )
    if hid_block % LANES or inp_block % LANES:
        own = jnp.concatenate([query_out_grads[0], query_inputs[0]], axis=1)
        return plain(own, *rest)
    train_h, train_i, basis_h, basis_i, eig_h, eig_i, query_ids, example_ids = map(vmem, rest)
    own_tokens = query_inputs.shape[1]
    width = query_out_grads.shape[2] + query_inputs.shape[2]
    tokens = own_tokens * shards
    own = jnp.concatenate([query_out_grads[0], query_inputs[0]], axis=1)
    own = call(
        hand_on_kernel,
        "hand_on",
        jax.ShapeDtypeStruct((own_tokens, width), jnp.bfloat16),
        flops=8_000_000_000,
    )(own)
    everyone, masks = gather(own, shards, by_kernel=True)
    small = jax.ShapeDtypeStruct((8, LANES), jnp.float32)
    own_self = call(
        self_kernel, "self_influence", small, flops=2 * 160 * 160 * 11264, moved=3_700_000
    )(train_h, train_i, eig_h, eig_i, example_ids)
    rotated = call(
        functools.partial(rotate_kernel, masks),
        "rotate",
        jax.ShapeDtypeStruct((1, tokens, hid_block + inp_block), jnp.bfloat16),
        flops=2 * 16 * 8_500_000,
        moved=17_000_000,
        scratch_shapes=[pltpu.VMEM((shards, own_tokens, width), jnp.bfloat16)],
    )(*everyone, basis_h, basis_i, eig_h, eig_i, own_self)
    parts, masks = gather(rotated[0], shards, ROTATED_PLAN)
    gram_shape = jax.ShapeDtypeStruct((2, tokens, train_h.shape[0]), jnp.float32)
    first, last = 3, 4
    grams, query_hot = call(
        functools.partial(early_kernel, masks[:first]),
        "early_grams",
        (gram_shape, jax.ShapeDtypeStruct((tokens, LANES), jnp.float32)),
        flops=500_000_000,
    )(*parts[:first], train_h, train_i, query_ids)
    grams = call(functools.partial(more_kernel, masks[first:last]), "more_grams", gram_shape, flops=300_000_000)(
        *parts[first:last], train_h, train_i, grams
    )
    mine = call(functools.partial(late_kernel, masks[last:]), "scores", small)(
        *parts[last:], train_h, train_i, grams, query_hot, example_ids, own_self
    )
    return call(
        finish_kernel,
        "finish",
        jax.ShapeDtypeStruct((E_DEV, QUERIES // 2), jnp.float32),
    )(mine, layer_swap(mine)).T


def plain(own, train_h, train_i, basis_h, basis_i, eig_h, eig_i, query_ids, example_ids):
    shards = lax.axis_size("ex")
    my_index = lax.axis_index("ex")
    width_h, hid_block = basis_h.shape
    inp_block = basis_i.shape[1]
    everyone = in_order(*gather(own, shards)).reshape(-1, own.shape[1])
    gain_h = 1.0 / (eig_h + DAMP)
    gain_i = 1.0 / (eig_i + DAMP)

    def rotate(tokens, basis, gain, block):
        product = jnp.dot(tokens, basis, preferred_element_type=jnp.float32)
        own_gain = lax.dynamic_slice_in_dim(gain, my_index * block, block, 1)
        return (product * own_gain).astype(jnp.bfloat16)

    rot_h = rotate(everyone[:, :width_h], basis_h, gain_h, hid_block)
    rot_i = rotate(everyone[:, width_h:], basis_i, gain_i, inp_block)
    pieces = in_order(*gather(jnp.concatenate([rot_h, rot_i], axis=1), shards))

    def gram(piece, train):
        split = train.reshape(train.shape[0], shards, -1)
        return jnp.einsum("nqf,tnf->qt", piece, split, preferred_element_type=jnp.float32)

    cross = gram(pieces[:, :, :hid_block], train_h) * gram(pieces[:, :, hid_block:], train_i)
    query_hot = query_ids == jnp.arange(QUERIES, dtype=jnp.int32)[:, None]
    example_hot = (example_ids == jnp.arange(E_DEV, dtype=jnp.int32)[:, None]).astype(jnp.float32)
    summed = jnp.dot(query_hot.astype(jnp.float32), cross, precision=lax.Precision.HIGHEST)
    scores = jnp.dot(summed, example_hot.T, precision=lax.Precision.HIGHEST)

    def pairs(train, gain):
        scaled = (train * gain).astype(jnp.bfloat16)
        return jnp.dot(scaled, train.T, preferred_element_type=jnp.float32)

    own_pairs = pairs(train_h, gain_h) * pairs(train_i, gain_i)
    sums = jnp.dot(example_hot, own_pairs, precision=lax.Precision.HIGHEST)
    own_self = jnp.sum(sums * example_hot, axis=1)
    mine = jnp.concatenate([scores, jnp.broadcast_to(own_self, scores.shape)], axis=1)
    total = mine + layer_swap(mine)
    half = QUERIES // 2
    total = lax.dynamic_slice_in_dim(total, lax.axis_index("layer") * half, half, 0)
    return total[:, :E_DEV] / jnp.sqrt(total[:, E_DEV:] + 1e-06)


def solution(mesh):
    in_specs = (
        P("layer", ("groups", "ex"), None),
        P("layer", ("groups", "ex"), None),
        P("layer", ("groups", "ex"), None),
        P("layer", ("groups", "ex"), None),
        P("layer", None, "ex"),
        P("layer", None, "ex"),
        P("layer", None),
        P("layer", None),
        P("groups"),
        P(("groups", "ex"), None),
    )
    out_specs = P(("groups", "layer"), "ex")
    return jax.shard_map(body, mesh=mesh, in_specs=in_specs, out_specs=out_specs, check_vma=False)
```
